256 devices in a mesh: tm: 16 (over x_lo, y, core), space: 16 (over z, x_hi).
Axes of the slice: x: 4 (x_hi: 2, x_lo: 2; x = x_hi * 2 + x_lo), y: 4, z: 8, core: 2. Of those that a mesh axis runs over, the one named last changes fastest.
Arguments:
- sources: float32 [4, 32, 32, 128, 128], P(None, 'tm', 'space'), may hold values from -6 to 6
- regions: int32 [128, 128], replicated, may hold values from 0 to 3
- material: float32 [3, 4], replicated, may hold values from 0.05 to 3, as said below
Outputs:
- response: float32 [4, 32, 32, 128, 128], P(None, 'tm', 'space')
The draws below stay inside these ranges and needn't reach their ends.
Inputs may be any that keep to these rules, and one draw needn't show every extreme that they name: `material`: row 0 (shear moduli) lies within 0.3 to 3.
All inputs are finite; a program needn't handle non-finite values.
Results may differ from the reference program's by a relative error of at most 0.00007.
Values sent between devices are 32-bit elements; how exact they have to be, the bound alone decides.
No kernel may reach another device: no remote copies, remote signals or barrier semaphores. Data moves between devices by JAX's collectives and lax.ppermute only.
A program may use at most 64 MiB of HBM per device.

```python
import jax
import jax.numpy as jnp
from jax import lax

NY = 128
NX = 128
FIELDS = 4
NCLASS = 4
SWEEPS = 4
STEPS = 32
PLANES = 32


def draw_material(key, part):
    key = jax.random.fold_in(key, 7)
    shear_key = jax.random.fold_in(key, 1)
    trans_key = jax.random.fold_in(key, 2)
    axial_key = jax.random.fold_in(key, 3)
    spread_key = jax.random.fold_in(key, 4)
    shear = 0.3 * jnp.exp(jax.random.uniform(shear_key, (1, NCLASS), jnp.float32) * jnp.log(10.0))
    order = jnp.stack([jax.random.permutation(trans_key, NCLASS), jax.random.permutation(axial_key, NCLASS)])
    stratum = order.astype(jnp.float32) + jax.random.uniform(spread_key, (2, NCLASS), jnp.float32)
    permeable = 0.05 * jnp.exp(stratum * (jnp.log(60.0) / NCLASS))
    return jnp.concatenate([shear, permeable], axis=0).astype(jnp.float32)


def place_ends(values, rng, low, largest):
    place = [jax.random.randint(jax.random.fold_in(rng, axis), (), 0, length) for axis, length in enumerate(values.shape)]
    main_axis = values.shape.index(max(values.shape))
    beside = place[:main_axis] + [(place[main_axis] + 1) % values.shape[main_axis]] + place[main_axis + 1:]
    return values.at[tuple(place)].set(low).at[tuple(beside)].set(largest)


def levels(rng, dims, pieces, least, largest):
    def one(position, blocks):
        steps = jax.random.uniform(jax.random.fold_in(jax.random.fold_in(rng, 6), position), (blocks,), jnp.float32, least / len(pieces), largest / len(pieces))
        return jnp.repeat(jnp.exp(steps), dims[position] // blocks).reshape((-1,) + (1,) * (len(dims) - position - 1))

    factor_of = one(*pieces[0])
    for cut in pieces[1:]:
        factor_of = factor_of * one(*cut)
    return factor_of


def bell_draw(own_key, dims, scale, bound, cuts=(), kind=jnp.bfloat16):
    level = levels(own_key, dims, cuts, -0.22, 0.18) if cuts else 1.0
    array = jax.random.normal(own_key, dims, jnp.float32) * scale * level
    return jnp.minimum(jnp.maximum(array, -bound), bound).astype(kind)


def setup_inputs(seed: int = 0) -> dict:
    splits = jax.random.split(jax.random.key(seed), 4)
    sources = bell_draw(splits[0], (FIELDS, STEPS, PLANES, NY, NX), 1.0, 6.0, ((1, 16), (2, 16)), jnp.float32)
    regions = place_ends(jax.random.randint(splits[1], (NY, NX), 0, NCLASS), jax.random.fold_in(splits[1], 1), 0, NCLASS - 1).astype(jnp.int32)
    material = draw_material(jax.random.fold_in(splits[3], 71), 0)
    return dict(sources=sources, regions=regions, material=material)


HIGHEST = lax.Precision.HIGHEST
BIOT_ALPHA = 0.6
STORAGE_COEF = 0.5
TIME_STEP = 0.5
RELAXATION = 0.8


def plane_faces(regions, material):
    classes = jnp.arange(material.shape[1], dtype=jnp.int32)
    onehot = (regions[None, :, :] == classes[:, None, None]).astype(jnp.float32)
    cell_value = jnp.sum(material[:, :, None, None] * onehot[None], axis=1)
    mean_cols = (cell_value[:, :, :-1] + cell_value[:, :, 1:]) * 0.5
    mean_rows = (cell_value[:, :-1, :] + cell_value[:, 1:, :]) * 0.5
    east_side = jnp.concatenate([mean_cols, cell_value[:, :, -1:]], axis=2)
    west_side = jnp.concatenate([cell_value[:, :, :1], mean_cols], axis=2)
    north_side = jnp.concatenate([mean_rows, cell_value[:, -1:, :]], axis=1)
    south_side = jnp.concatenate([cell_value[:, :1, :], mean_rows], axis=1)
    return jnp.stack([east_side, west_side, north_side, south_side, cell_value])


def dft_tables(cycle_len):
    counter = jnp.arange(cycle_len, dtype=jnp.int32)
    phases = ((counter[:, None] * counter[None, :]) % cycle_len).astype(jnp.float32) * (2.0 * jnp.pi / cycle_len)
    return jnp.cos(phases), jnp.sin(phases)


def shift_factors(frequency, cycle_len):
    phases = (frequency % cycle_len).astype(jnp.float32) * (2.0 * jnp.pi / cycle_len)
    return 1.0 - jnp.cos(phases), jnp.sin(phases)


def to_spectrum(portion, cosine, sine_table):
    real_part = jnp.einsum('kt,ctzyx->ckzyx', cosine, portion, precision=HIGHEST)
    imag_part = -jnp.einsum('kt,ctzyx->ckzyx', sine_table, portion, precision=HIGHEST)
    return jnp.stack([real_part, imag_part], axis=1)


def to_samples(spectral, cosine, sine_table):
    cycle_len = spectral.shape[2]
    summed = jnp.einsum('kt,ckzyx->ctzyx', cosine, spectral[:, 0], precision=HIGHEST) - jnp.einsum('kt,ckzyx->ctzyx', sine_table, spectral[:, 1], precision=HIGHEST)
    return summed / cycle_len


def operate(padded, face_table, lam_real, lam_imag):
    centre = padded[..., 1:-1, 1:-1, 1:-1]
    east_side = padded[..., 1:-1, 1:-1, 2:]
    west_side = padded[..., 1:-1, 1:-1, :-2]
    north_side = padded[..., 1:-1, 2:, 1:-1]
    south_side = padded[..., 1:-1, :-2, 1:-1]
    upward = padded[..., 2:, 1:-1, 1:-1]
    downward = padded[..., :-2, 1:-1, 1:-1]
    shear = face_table[:, 0]
    kappa_side = face_table[:4, 1]
    kappa_axis = face_table[4, 2]
    shear_diag = shear[0] + shear[1] + shear[2] + shear[3] + 2.0 * shear[4]
    kappa_diag = kappa_side[0] + kappa_side[1] + kappa_side[2] + kappa_side[3] + 2.0 * kappa_axis
    elastic = shear[0] * east_side[:3] + shear[1] * west_side[:3] + shear[2] * north_side[:3] + shear[3] * south_side[:3] + shear[4] * (upward[:3] + downward[:3])
    gradient = 0.5 * jnp.stack([east_side[3] - west_side[3], north_side[3] - south_side[3], upward[3] - downward[3]])
    momentum = shear_diag * centre[:3] - elastic + BIOT_ALPHA * gradient
    divergence = 0.5 * ((east_side[0] - west_side[0]) + (north_side[1] - south_side[1]) + (upward[2] - downward[2]))
    flow_sum = kappa_side[0] * east_side[3] + kappa_side[1] * west_side[3] + kappa_side[2] * north_side[3] + kappa_side[3] * south_side[3] + kappa_axis * (upward[3] + downward[3])
    content = BIOT_ALPHA * divergence + STORAGE_COEF * centre[3]
    lam_r = lam_real[:, None, None, None]
    lam_i = lam_imag[:, None, None, None]
    rate_term = jnp.stack([lam_r * content[0] - lam_i * content[1], lam_r * content[1] + lam_i * content[0]])
    pressure = rate_term + TIME_STEP * (kappa_diag * centre[3] - flow_sum)
    return jnp.concatenate([momentum, pressure[None]], axis=0)


def smooth(source_hat, face_table, lam_real, lam_imag, add_rims):
    shear = face_table[:, 0]
    kappa_side = face_table[:4, 1]
    kappa_axis = face_table[4, 2]
    shear_diag = shear[0] + shear[1] + shear[2] + shear[3] + 2.0 * shear[4]
    kappa_diag = kappa_side[0] + kappa_side[1] + kappa_side[2] + kappa_side[3] + 2.0 * kappa_axis
    diag_real = STORAGE_COEF * lam_real[:, None, None, None] + TIME_STEP * kappa_diag
    diag_imag = STORAGE_COEF * lam_imag[:, None, None, None]
    modulus = diag_real * diag_real + diag_imag * diag_imag

    def scaled(residual):
        moment = residual[:3] / shear_diag
        quot_real = (residual[3, 0] * diag_real + residual[3, 1] * diag_imag) / modulus
        quot_imag = (residual[3, 1] * diag_real - residual[3, 0] * diag_imag) / modulus
        return jnp.concatenate([moment, jnp.stack([quot_real, quot_imag])[None]], axis=0)

    iterate = RELAXATION * scaled(source_hat)
    for sweep_index in range(SWEEPS - 1):
        residual = source_hat - operate(add_rims(iterate), face_table, lam_real, lam_imag)
        iterate = iterate + RELAXATION * scaled(residual)
    return iterate


def reference(sources, regions, material):
    cosine, sine_table = dft_tables(STEPS)
    face_table = plane_faces(regions, material)
    spectral = jnp.moveaxis(to_spectrum(sources, cosine, sine_table), 2, 0)
    lam_real, lam_imag = shift_factors(jnp.arange(STEPS, dtype=jnp.int32), STEPS)

    def add_rims(iterate):
        return jnp.pad(iterate, ((0, 0), (0, 0), (0, 0), (1, 1), (1, 1), (1, 1)))

    def solve_one(packed):
        source_hat, lam_r, lam_i = packed
        return smooth(source_hat[:, :, None], face_table, lam_r[None], lam_i[None], add_rims)[:, :, 0]

    solved = lax.map(solve_one, (spectral, lam_real, lam_imag))
    return to_samples(jnp.moveaxis(solved, 0, 2), cosine, sine_table)
```

```python
import functools
import math

import jax
import jax.numpy as jnp
import numpy as np
from jax import lax
from jax.experimental import pallas as pl
from jax.experimental.pallas import tpu as pltpu
from jax.sharding import Mesh
from jax.sharding import PartitionSpec as P

AXES = ("xl", "y", "c", "z", "xh")
SIZES = dict(xl=2, y=4, c=2, z=8, xh=2)
LEVEL = ("xl", "y", "c", "xh")
STEPS = 32
PAIRS = 16
FIELDS = 4
MIB = 1 << 20


def chip_at(pos):
    y, x = divmod(pos, 4)
    return (3 - x if y % 2 else x), y


def level_index(pos, core):
    x, y = chip_at(pos)
    return ((((x % 2) * 4 + y) * 2 + core) * 2) + x // 2


def device_index(z, block):
    x, y = chip_at(block // 2)
    return ((((x % 2) * 4 + y) * 2 + block % 2) * 8 + z) * 2 + x // 2


def shift(dz, db):
    return [
        (device_index(z, b), device_index(z + dz, b + db))
        for z in range(8)
        for b in range(32)
        if 0 <= z + dz < 8 and 0 <= b + db < 32
    ]


def rows():
    return lax.broadcasted_iota(jnp.int32, (8, 128), 0)


def lanes():
    return lax.broadcasted_iota(jnp.int32, (8, 128), 1)


def among(index, members):
    mask = index == members[0]
    for member in members[1:]:
        mask = mask | (index == member)
    return mask


def roll(tile, amount):
    amount %= 8
    return tile if amount == 0 else pltpu.roll(tile, amount, 0)


def mul_const(re, im, cr, ci):
    def axpy(a, x, b, y):
        terms = []
        for k, v in ((a, x), (b, y)):
            if abs(k) > 1e-12:
                terms.append((k, v))
        total = None
        for k, v in terms:
            if total is None:
                total = v if abs(k - 1) < 1e-12 else (-v if abs(k + 1) < 1e-12 else v * np.float32(k))
            elif abs(k - 1) < 1e-12:
                total = total + v
            elif abs(k + 1) < 1e-12:
                total = total - v
            else:
                total = total + v * np.float32(k)
        return total

    if abs(abs(cr) - abs(ci)) < 1e-12:
        root = np.float32(abs(cr))
        sr, si = math.copysign(1, cr), math.copysign(1, ci)
        return axpy(sr, re * root, -si, im * root), axpy(si, re * root, sr, im * root)
    return axpy(cr, re, -ci, im), axpy(ci, re, cr, im)


def rfft(x):
    n = len(x)
    if n == 2:
        return [(x[0] + x[1], None), (x[0] - x[1], None)]
    even, odd = rfft(x[0::2]), rfft(x[1::2])
    out = [None] * (n // 2 + 1)
    out[0] = (even[0][0] + odd[0][0], None)
    out[n // 2] = (even[0][0] - odd[0][0], None)
    out[n // 4] = (even[n // 4][0], -odd[n // 4][0])
    for k in range(1, n // 4):
        angle = -2 * math.pi * k / n
        tr, ti = mul_const(*odd[k], math.cos(angle), math.sin(angle))
        er, ei = even[k]
        out[k] = (er + tr, ei + ti)
        out[n // 2 - k] = (er - tr, ti - ei)
    return out


def irfft(spec):
    n = 2 * (len(spec) - 1)
    if n == 2:
        return [spec[0][0] + spec[1][0], spec[0][0] - spec[1][0]]
    q = n // 4
    even, odd = [None] * (q + 1), [None] * (q + 1)
    even[0] = (spec[0][0] + spec[2 * q][0], None)
    odd[0] = (spec[0][0] - spec[2 * q][0], None)
    even[q] = (2.0 * spec[q][0], None)
    odd[q] = (-2.0 * spec[q][1], None)
    for k in range(1, q):
        ar, ai = spec[k]
        br, bi = spec[2 * q - k]
        even[k] = (ar + br, ai - bi)
        angle = 2 * math.pi * k / n
        odd[k] = mul_const(ar - br, ai + bi, math.cos(angle), math.sin(angle))
    a, b = irfft(even), irfft(odd)
    return [v for two in zip(a, b) for v in two]


def split_kernel(src, out):
    upper = rows() < 4

    def body(i, _):
        f, t = i // 2, i % 2
        for pos in range(16):
            a = src[f, t, 0, pl.ds(8 * pos, 8), :]
            b = src[f, t, 1, pl.ds(8 * pos, 8), :]
            out[level_index(pos, 0), f, t] = jnp.where(upper, a, roll(b, 4))
            out[level_index(pos, 1), f, t] = jnp.where(upper, roll(a, 4), b)
        return 0

    lax.fori_loop(0, 8, body, 0)


def join_kernel(src, out):
    upper = rows() < 4

    def body(i, _):
        f, t = i // 2, i % 2
        for pos in range(16):
            a = src[level_index(pos, 0), f, t]
            b = src[level_index(pos, 1), f, t]
            out[f, t, 0, pl.ds(8 * pos, 8), :] = jnp.where(upper, a, roll(b, 4))
            out[f, t, 1, pl.ds(8 * pos, 8), :] = jnp.where(upper, roll(a, 4), b)
        return 0

    lax.fori_loop(0, 8, body, 0)


def spectrum_kernel(src, own, zup, zdn):
    upper = rows() < 4

    def body(f, _):
        for half in range(2):
            spec = rfft([src[(t // 2) * 2 + half, f, t % 2] for t in range(STEPS)])
            pairs = [(spec[0][0], spec[16][0])] + spec[1:16]
            for q, (re, im) in enumerate(pairs):
                own[q, half, f, 0] = re
                own[q, half, f, 1] = im
                if half == 0:
                    zdn[q, f, 0] = re
                    zdn[q, f, 1] = im
                    zup[q, f, 2] = jnp.where(upper, roll(re, 4), im)
                else:
                    zup[q, f, 0] = re
                    zup[q, f, 1] = im
                    zdn[q, f, 2] = jnp.where(upper, re, roll(im, 4))
        return 0

    lax.fori_loop(0, FIELDS, body, 0)


def corner_kernel(zlo, zhi, cup, cdn):
    r = rows()
    for_up = among(r, (3, 6, 7))
    for_dn = among(r, (0, 4, 5))

    def body(q, _):
        for f in range(FIELDS):
            for c in range(2):
                low = zlo[q, f, c]
                high = roll(zhi[q, f, c], 2)
                cup[q, f, c] = jnp.where(for_up, low, high)
                cdn[q, f, c] = jnp.where(for_dn, low, high)
        return 0

    lax.fori_loop(0, PAIRS, body, 0)


(A, AE, AW, AN, AS, AC, GE, GW, G, KE, KW, KN, KS, KZ, HKD, VALID) = range(16)


def solve_kernel(flags, lam, coef, edge, own, rlo, rhi, zlo, zhi, clo, chi, out, x0, x0e, x1, x2, sol):
    r, l = rows(), lanes()
    middle = among(r, (2, 3, 4, 5))
    upper = r < 4
    first, last = r == 0, r == 7
    east = jnp.where(l == 127, 0.0, 0.3).astype(jnp.float32)
    west = jnp.where(l == 0, 0.0, 0.3).astype(jnp.float32)
    near_low = among(r, (2, 3, 6, 7))
    far_low = among(r, (1, 5))
    pick_lo = among(r, (3, 6, 7))
    pick_hi = among(r, (1, 4, 5))

    def pair(q, _):
        m00, m11, m01 = lam[q, 0], lam[q, 1], lam[q, 2]
        di = -0.5 * m01

        def inverse(hkd, valid):
            d0, d1 = hkd + 0.5 * m00, hkd + 0.5 * m11
            inv = 0.8 * valid / (d0 * d1 + di * di)
            return inv * d1, inv * d0, inv * di

        pa, pb, pc = inverse(coef[HKD], coef[VALID])
        ea, eb, ec = inverse(edge[1], edge[2])

        def scale(dest, plane, f, tiles, a, b00, b11, b01):
            re, im = tiles
            if f < 3:
                dest[plane, f, 0] = a * re
                dest[plane, f, 1] = a * im
            else:
                dest[plane, f, 0] = b00 * re + b01 * im
                dest[plane, f, 1] = b11 * im - b01 * re

        a_mid, a_edge = coef[A], edge[0]
        for f in range(FIELDS):
            planes = [[None, None] for _ in range(10)]
            edges = [[None, None] for _ in range(4)]
            for c in range(2):
                for half in range(2):
                    centre = own[q, half, f, c]
                    low, high = rlo[q, half, f, c], rhi[q, half, f, c]
                    near = jnp.where(near_low, low, high)
                    far = jnp.where(far_low, low, high)
                    for odd in range(2):
                        p = 2 * half + odd
                        inner, outer = (6, 2) if odd else (2, 6)
                        planes[3 + p][c] = jnp.where(middle, roll(centre, inner), roll(near, outer))
                        edges[p][c] = roll(far, outer)
                cu, cd = clo[q, f, c], chi[q, f, c]
                lo, hi = zlo[q, f, c], zhi[q, f, c]
                g1 = jnp.where(pick_lo, cu, cd)
                g2 = jnp.where(pick_hi, cu, cd)
                planes[2][c] = jnp.where(middle, roll(lo, 6), roll(g1, 2))
                planes[1][c] = jnp.where(middle, roll(lo, 2), roll(g1, 6))
                planes[7][c] = jnp.where(middle, roll(hi, 2), roll(g2, 4))
                planes[8][c] = jnp.where(middle, roll(hi, 6), g2)
            lo, hi = zlo[q, f, 2], zhi[q, f, 2]
            planes[0] = [roll(lo, 2), roll(lo, 6)]
            planes[9] = [roll(hi, 2), roll(hi, 6)]
            for p in range(10):
                scale(x0, p, f, planes[p], a_mid, pa, pb, pc)
            for p in range(4):
                scale(x0e, p, f, edges[p], a_edge, ea, eb, ec)

        def update(src, at, plane, base, edges=None):
            new = [[None, None] for _ in range(FIELDS)]
            div, flow = [None, None], [None, None]
            for c in range(2):
                cur = [src[plane - at, f, c] for f in range(FIELDS)]
                up = [src[plane - at + 1, f, c] for f in range(FIELDS)]
                dn = [src[plane - at - 1, f, c] for f in range(FIELDS)]
                es = [pltpu.roll(v, 127, 1) for v in cur]
                ws = [pltpu.roll(v, 1, 1) for v in cur]
                if edges is None:
                    ns = [roll(v, 7) for v in cur]
                    ss = [roll(v, 1) for v in cur]
                else:
                    ed = [x0e[edges, f, c] for f in range(FIELDS)]
                    ns = [roll(jnp.where(first, e, v), 7) for e, v in zip(ed, cur)]
                    ss = [roll(jnp.where(last, e, v), 1) for e, v in zip(ed, cur)]
                grad = [
                    coef[GE] * es[3] - coef[GW] * ws[3],
                    coef[G] * (ns[3] - ss[3]),
                    coef[G] * (up[3] - dn[3]),
                ]
                for f in range(3):
                    v = base(plane, f, c, cur[f])
                    v = v + coef[AE] * es[f] + coef[AW] * ws[f]
                    v = v + coef[AN] * ns[f] + coef[AS] * ss[f]
                    new[f][c] = v + coef[AC] * (up[f] + dn[f]) - grad[f]
                flow[c] = (
                    coef[KE] * es[3]
                    + coef[KW] * ws[3]
                    + coef[KN] * ns[3]
                    + coef[KS] * ss[3]
                    + coef[KZ] * (up[3] + dn[3])
                )
                div[c] = east * es[0] - west * ws[0] + 0.3 * ((ns[1] - ss[1]) + (up[2] - dn[2]))
                new[3][c] = base(plane, 3, c, cur[3])
            g0 = flow[0] - (m00 * div[0] + m01 * div[1])
            g1 = flow[1] - (m11 * div[1] - m01 * div[0])
            new[3][0] = new[3][0] + pa * g0 + pc * g1
            new[3][1] = new[3][1] + pb * g1 - pc * g0
            return new

        def later(plane, f, c, cur):
            return x0[plane, f, c] + 0.2 * cur

        def sweep(src, at, dest, dest_at, low, high, base, with_edges):
            for plane in range(low, high):
                inside = 3 <= plane <= 6
                new = update(src, at, plane, base, plane - 3 if with_edges and inside else None)
                keep = flags[0] if plane < 3 else flags[1]
                for f in range(FIELDS):
                    for c in range(2):
                        dest[plane - dest_at, f, c] = new[f][c] if inside else keep * new[f][c]

        sweep(x0, 0, x1, 1, 1, 9, lambda plane, f, c, cur: 1.2 * cur, True)
        sweep(x1, 1, x2, 2, 2, 8, later, False)
        for half in range(2):
            one = update(x2, 2, 3 + 2 * half, later)
            two = update(x2, 2, 4 + 2 * half, later)
            for f in range(FIELDS):
                for c in range(2):
                    sol[q, half, f, c] = jnp.where(upper, roll(one[f][c], 6), roll(two[f][c], 2))
        return 0

    lax.fori_loop(0, PAIRS, pair, 0)

    scale32 = np.float32(1.0 / STEPS)

    def back(f, _):
        for half in range(2):
            tiles = [
                (sol[q, half, f, 0] * scale32, sol[q, half, f, 1] * scale32) for q in range(PAIRS)
            ]
            spec = [(tiles[0][0], None)] + tiles[1:] + [(tiles[0][1], None)]
            for t, v in enumerate(irfft(spec)):
                out[(t // 2) * 2 + half, f, t % 2] = v
        return 0

    lax.fori_loop(0, FIELDS, back, 0)


def call(kernel, outs, in_spaces, scratch=(), limit=16):
    f32 = jnp.float32
    shapes = [jax.ShapeDtypeStruct(s, f32) for s in outs]
    specs = [pl.BlockSpec(memory_space=pltpu.VMEM) for _ in outs]
    single = len(outs) == 1
    return pl.pallas_call(
        kernel,
        out_shape=shapes[0] if single else shapes,
        in_specs=[pl.BlockSpec(memory_space=m) for m in in_spaces],
        out_specs=specs[0] if single else specs,
        scratch_shapes=[pltpu.VMEM(s, f32) for s in scratch],
        compiler_params=pltpu.CompilerParams(vmem_limit_bytes=limit * MIB),
    )


def coefficients(regions, material, block):
    classes = jnp.arange(material.shape[1], dtype=jnp.int32)
    onehot = (regions[None, :, :] == classes[:, None, None]).astype(jnp.float32)
    value = jnp.sum(material[:, :, None, None] * onehot[None], axis=1)
    mean_cols = (value[:, :, :-1] + value[:, :, 1:]) * 0.5
    mean_rows = (value[:, :-1, :] + value[:, 1:, :]) * 0.5
    e = jnp.concatenate([mean_cols, value[:, :, -1:]], axis=2)
    w = jnp.concatenate([value[:, :, :1], mean_cols], axis=2)
    n = jnp.concatenate([mean_rows, value[:, -1:, :]], axis=1)
    s = jnp.concatenate([value[:, :1, :], mean_rows], axis=1)
    shear_diag = e[0] + w[0] + n[0] + s[0] + 2.0 * value[0]
    kappa_diag = e[1] + w[1] + n[1] + s[1] + 2.0 * value[2]
    column = jnp.arange(128, dtype=jnp.int32)[None, :]
    has_e = (column < 127).astype(jnp.float32)
    has_w = (column > 0).astype(jnp.float32)
    a = 0.8 / shear_diag
    one = jnp.ones_like(a)
    table = jnp.stack(
        [
            a, a * e[0] * has_e, a * w[0] * has_w, a * n[0], a * s[0], a * value[0],
            0.3 * a * has_e, 0.3 * a * has_w, 0.3 * a,
            0.5 * e[1] * has_e, 0.5 * w[1] * has_w, 0.5 * n[1], 0.5 * s[1], 0.5 * value[2],
            0.5 * kappa_diag, one,
        ]
    )
    pad = jnp.zeros((16, 4, 128), jnp.float32).at[HKD].set(1.0)
    table = jnp.concatenate([pad, table, pad], axis=1)
    window = lax.dynamic_slice_in_dim(table, 4 * block + 1, 10, axis=1)
    few = jnp.stack([window[A], window[HKD], window[VALID]])
    edge = jnp.concatenate([few[:, 9:10], few[:, 1:7], few[:, 0:1]], axis=1)
    return window[:, 1:9], edge


def lam_table():
    k = np.arange(1, PAIRS)
    real, imag = 1 - np.cos(2 * np.pi * k / STEPS), np.sin(2 * np.pi * k / STEPS)
    rest = np.stack([real, real, -imag], axis=1)
    return np.concatenate([[[0.0, 2.0, 0.0]], rest]).astype(np.float32)


def on_device(sources, regions, material):
    vmem, smem = pltpu.VMEM, pltpu.SMEM
    x = lax.axis_index("xh") * 2 + lax.axis_index("xl")
    y = lax.axis_index("y")
    z = lax.axis_index("z")
    pos = y * 4 + jnp.where(y % 2 == 1, 3 - x, x)
    block = 2 * pos + lax.axis_index("c")
    piece = (32, FIELDS, 2, 8, 128)

    def level(v):
        return lax.all_to_all(v, LEVEL, 0, 0, tiled=True)

    def move(v, dz, db):
        return lax.ppermute(v, AXES, shift(dz, db))

    arrived = level(call(split_kernel, [piece], [vmem])(sources))
    own, zup, zdn = call(
        spectrum_kernel,
        [(PAIRS, 2, FIELDS, 2, 8, 128), (PAIRS, FIELDS, 3, 8, 128), (PAIRS, FIELDS, 3, 8, 128)],
        [vmem],
    )(arrived)
    zlo, zhi = move(zup, 1, 0), move(zdn, -1, 0)
    rlo, rhi = move(own, 0, 1), move(own, 0, -1)
    cup, cdn = call(corner_kernel, [(PAIRS, FIELDS, 2, 8, 128)] * 2, [vmem, vmem])(zlo, zhi)
    clo, chi = move(cup, 0, 1), move(cdn, 0, -1)
    coef, edge = coefficients(regions, material, block)
    flags = jnp.stack([(z > 0), (z < 7)]).astype(jnp.float32)
    answer = call(
        solve_kernel,
        [piece],
        [smem, smem] + [vmem] * 9,
        scratch=[
            (10, FIELDS, 2, 8, 128),
            (4, FIELDS, 2, 8, 128),
            (8, FIELDS, 2, 8, 128),
            (6, FIELDS, 2, 8, 128),
            (PAIRS, 2, FIELDS, 2, 8, 128),
        ],
        limit=24,
    )(flags, jnp.asarray(lam_table()), coef, edge, own, rlo, rhi, zlo, zhi, clo, chi)
    return call(join_kernel, [(FIELDS, 2, 2, 128, 128)], [vmem])(level(answer))


def solution(mesh):
    fine = Mesh(mesh.devices.reshape([SIZES[a] for a in AXES]), AXES)
    spec = P(None, ("xl", "y", "c"), ("z", "xh"), None, None)
    return jax.shard_map(
        on_device, mesh=fine, in_specs=(spec, P(), P()), out_specs=spec, check_vma=False
    )
```

```python
import functools
import math

import jax
import jax.numpy as jnp
import numpy as np
from jax import lax
from jax.experimental import pallas as pl
from jax.experimental.pallas import tpu as pltpu
from jax.sharding import Mesh
from jax.sharding import PartitionSpec as P

AXES = ("xl", "y", "c", "z", "xh")
SIZES = dict(xl=2, y=4, c=2, z=8, xh=2)
LEVEL = ("xl", "y", "c", "xh")
STEPS = 32
PAIRS = 16
FIELDS = 4
MIB = 1 << 20


def chip_at(pos):
    y, x = divmod(pos, 4)
    return (3 - x if y % 2 else x), y


def level_index(pos, core):
    x, y = chip_at(pos)
    return ((((x % 2) * 4 + y) * 2 + core) * 2) + x // 2


def device_index(z, block):
    x, y = chip_at(block // 2)
    return ((((x % 2) * 4 + y) * 2 + block % 2) * 8 + z) * 2 + x // 2


def level_swap(parity):
    low = [z for z in range(7) if z % 2 == parity]
    up = [(device_index(z, b), device_index(z + 1, b)) for z in low for b in range(32)]
    return up + [(t, s) for s, t in up]


def block_swap(parity):
    low = [b for b in range(31) if b % 2 == parity]
    up = [(device_index(z, b), device_index(z, b + 1)) for z in range(8) for b in low]
    return up + [(t, s) for s, t in up]


def rows():
    return lax.broadcasted_iota(jnp.int32, (8, 128), 0)


def lanes():
    return lax.broadcasted_iota(jnp.int32, (8, 128), 1)


def among(index, members):
    mask = index == members[0]
    for member in members[1:]:
        mask = mask | (index == member)
    return mask


def roll(tile, amount):
    amount %= 8
    return tile if amount == 0 else pltpu.roll(tile, amount, 0)


def mul_const(re, im, cr, ci):
    def axpy(a, x, b, y):
        terms = []
        for k, v in ((a, x), (b, y)):
            if abs(k) > 1e-12:
                terms.append((k, v))
        total = None
        for k, v in terms:
            if total is None:
                total = v if abs(k - 1) < 1e-12 else (-v if abs(k + 1) < 1e-12 else v * np.float32(k))
            elif abs(k - 1) < 1e-12:
                total = total + v
            elif abs(k + 1) < 1e-12:
                total = total - v
            else:
                total = total + v * np.float32(k)
        return total

    if abs(abs(cr) - abs(ci)) < 1e-12:
        root = np.float32(abs(cr))
        sr, si = math.copysign(1, cr), math.copysign(1, ci)
        return axpy(sr, re * root, -si, im * root), axpy(si, re * root, sr, im * root)
    return axpy(cr, re, -ci, im), axpy(ci, re, cr, im)


def rfft(x):
    n = len(x)
    if n == 2:
        return [(x[0] + x[1], None), (x[0] - x[1], None)]
    even, odd = rfft(x[0::2]), rfft(x[1::2])
    out = [None] * (n // 2 + 1)
    out[0] = (even[0][0] + odd[0][0], None)
    out[n // 2] = (even[0][0] - odd[0][0], None)
    out[n // 4] = (even[n // 4][0], -odd[n // 4][0])
    for k in range(1, n // 4):
        angle = -2 * math.pi * k / n
        tr, ti = mul_const(*odd[k], math.cos(angle), math.sin(angle))
        er, ei = even[k]
        out[k] = (er + tr, ei + ti)
        out[n // 2 - k] = (er - tr, ti - ei)
    return out


def irfft(spec):
    n = 2 * (len(spec) - 1)
    if n == 2:
        return [spec[0][0] + spec[1][0], spec[0][0] - spec[1][0]]
    q = n // 4
    even, odd = [None] * (q + 1), [None] * (q + 1)
    even[0] = (spec[0][0] + spec[2 * q][0], None)
    odd[0] = (spec[0][0] - spec[2 * q][0], None)
    even[q] = (2.0 * spec[q][0], None)
    odd[q] = (-2.0 * spec[q][1], None)
    for k in range(1, q):
        ar, ai = spec[k]
        br, bi = spec[2 * q - k]
        even[k] = (ar + br, ai - bi)
        angle = 2 * math.pi * k / n
        odd[k] = mul_const(ar - br, ai + bi, math.cos(angle), math.sin(angle))
    a, b = irfft(even), irfft(odd)
    return [v for two in zip(a, b) for v in two]


def split_kernel(src, out):
    upper = rows() < 4

    def body(i, _):
        f, t = i // 2, i % 2
        for pos in range(16):
            a = src[f, t, 0, pl.ds(8 * pos, 8), :]
            b = src[f, t, 1, pl.ds(8 * pos, 8), :]
            out[level_index(pos, 0), f, t] = jnp.where(upper, a, roll(b, 4))
            out[level_index(pos, 1), f, t] = jnp.where(upper, roll(a, 4), b)
        return 0

    lax.fori_loop(0, 8, body, 0)


def join_kernel(src, out):
    upper = rows() < 4

    def body(i, _):
        f, t = i // 2, i % 2
        for pos in range(16):
            a = src[level_index(pos, 0), f, t]
            b = src[level_index(pos, 1), f, t]
            out[f, t, 0, pl.ds(8 * pos, 8), :] = jnp.where(upper, a, roll(b, 4))
            out[f, t, 1, pl.ds(8 * pos, 8), :] = jnp.where(upper, roll(a, 4), b)
        return 0

    lax.fori_loop(0, 8, body, 0)


def spectrum_kernel(place, src, own, even, odd):
    r = rows()
    upper = r < 4
    on_even = (r * 0 + place[0]) == 0

    def body(f, _):
        for half in range(2):
            spec = rfft([src[(t // 2) * 2 + half, f, t % 2] for t in range(STEPS)])
            pairs = [(spec[0][0], spec[16][0])] + spec[1:16]
            for q in range(PAIRS):
                for c in range(2):
                    own[q, half, f, c] = pairs[q][c]
        return 0

    lax.fori_loop(0, FIELDS, body, 0)

    def messages(q, _):
        for f in range(FIELDS):
            low = [own[q, 0, f, c] for c in range(2)]
            high = [own[q, 1, f, c] for c in range(2)]
            up = high + [jnp.where(upper, roll(low[0], 4), low[1])]
            down = low + [jnp.where(upper, high[0], roll(high[1], 4))]
            for n in range(3):
                even[q, f, n] = jnp.where(on_even, up[n], down[n])
                odd[q, f, n] = jnp.where(on_even, down[n], up[n])
        return 0

    lax.fori_loop(0, PAIRS, messages, 0)


def corner_kernel(place, even, odd, inside, across):
    r = rows()
    on_even = (r * 0 + place[0]) == 0
    for_next = jnp.where(among(r, (3, 6, 7)), 1, 0)
    for_last = jnp.where(among(r, (0, 4, 5)), 1, 0)
    first_core = (r * 0 + place[1]) == 0
    for_inside = jnp.where(first_core, for_next, for_last) == 1
    for_across = jnp.where(first_core, for_last, for_next) == 1

    def body(q, _):
        for f in range(FIELDS):
            for c in range(2):
                a, b = even[q, f, c], odd[q, f, c]
                low = jnp.where(on_even, b, a)
                high = roll(jnp.where(on_even, a, b), 2)
                inside[q, f, c] = jnp.where(for_inside, low, high)
                across[q, f, c] = jnp.where(for_across, low, high)
        return 0

    lax.fori_loop(0, PAIRS, body, 0)


(A, AE, AW, AN, AS, AC, GE, GW, G, KE, KW, KN, KS, KZ, HKD, VALID) = range(16)


def coefficient_kernel(first_row, material, near, coef, edge):
    shape = (16, 128)
    line = first_row[0] - 4 + lax.broadcasted_iota(jnp.int32, shape, 0)
    column = lax.broadcasted_iota(jnp.int32, shape, 1)
    there = [column < 127, column > 0, line < 127, line > 0]
    has_e, has_w = [jnp.where(t, 1.0, 0.0).astype(jnp.float32) for t in there[:2]]
    valid = jnp.where((line >= 0) & (line <= 127), 1.0, 0.0).astype(jnp.float32)
    classes = near[...]

    def parts(row):
        value = jnp.zeros(shape, jnp.float32)
        for m in range(4):
            value = jnp.where(classes == m, material[row, m], value)
        moved = [pltpu.roll(value, 127, 1), pltpu.roll(value, 1, 1), pltpu.roll(value, 15, 0), pltpu.roll(value, 1, 0)]
        return value, [jnp.where(t, (value + v) * 0.5, value) for t, v in zip(there, moved)]

    shear, (se, sw, sn, ss) = parts(0)
    _, (ke, kw, kn, ks) = parts(1)
    axial, _ = parts(2)
    a = 0.8 * valid / (se + sw + sn + ss + 2.0 * shear)
    half = 0.5 * valid
    table = [
        a, a * se * has_e, a * sw * has_w, a * sn, a * ss, a * shear,
        0.3 * a * has_e, 0.3 * a * has_w, 0.3 * a,
        half * ke * has_e, half * kw * has_w, half * kn, half * ks, half * axial,
        0.5 * (ke + kw + kn + ks + 2.0 * axial), valid,
    ]
    for n, v in enumerate(table):
        turned = pltpu.roll(v, 14, 0)
        coef[n] = turned[:8]
        if n in (A, HKD, VALID):
            edge[(A, HKD, VALID).index(n)] = turned[8:]


def inverse_diagonal(lam, q, half_diag, valid):
    d0, d1, di = half_diag + 0.5 * lam[q, 0], half_diag + 0.5 * lam[q, 1], -0.5 * lam[q, 2]
    inv = 0.8 * valid / (d0 * d1 + di * di)
    return inv * d1, inv * d0, inv * di


def first_iterate(f, tiles, a, diagonal):
    re, im = tiles
    if f < 3:
        return a * re, a * im
    b00, b11, b01 = diagonal
    return b00 * re + b01 * im, b11 * im - b01 * re


def updater(lam, q, coef, diagonal):
    l = lanes()
    east = jnp.where(l == 127, 0.0, 0.3).astype(jnp.float32)
    west = jnp.where(l == 0, 0.0, 0.3).astype(jnp.float32)
    m00, m11, m01 = lam[q, 0], lam[q, 1], lam[q, 2]
    pa, pb, pc = diagonal

    def update(cur, up, dn, base, north=None, south=None):
        north, south = north or cur, south or cur
        new = [[None, None] for _ in range(FIELDS)]
        div, flow = [None, None], [None, None]
        for c in range(2):
            es = [pltpu.roll(cur[f][c], 127, 1) for f in range(FIELDS)]
            ws = [pltpu.roll(cur[f][c], 1, 1) for f in range(FIELDS)]
            ns = [roll(north[f][c], 7) for f in range(FIELDS)]
            ss = [roll(south[f][c], 1) for f in range(FIELDS)]
            grad = [
                coef[GE] * es[3] - coef[GW] * ws[3],
                coef[G] * (ns[3] - ss[3]),
                coef[G] * (up[3][c] - dn[3][c]),
            ]
            for f in range(3):
                v = base(f, c) + coef[AE] * es[f] + coef[AW] * ws[f]
                v = v + coef[AN] * ns[f] + coef[AS] * ss[f]
                new[f][c] = v + coef[AC] * (up[f][c] + dn[f][c]) - grad[f]
            flow[c] = (
                coef[KE] * es[3]
                + coef[KW] * ws[3]
                + coef[KN] * ns[3]
                + coef[KS] * ss[3]
                + coef[KZ] * (up[3][c] + dn[3][c])
            )
            div[c] = east * es[0] - west * ws[0] + 0.3 * ((ns[1] - ss[1]) + (up[2][c] - dn[2][c]))
        g0 = flow[0] - (m00 * div[0] + m01 * div[1])
        g1 = flow[1] - (m11 * div[1] - m01 * div[0])
        new[3][0] = base(3, 0) + pa * g0 + pc * g1
        new[3][1] = base(3, 1) + pb * g1 - pc * g0
        return new

    return update


def plane(ref, *index):
    return [[ref[(*index, f, c)] for c in range(2)] for f in range(FIELDS)]


def inner_kernel(place, lam, coef, edge, own, inside, across, x0, x1):
    r = rows()
    middle = among(r, (2, 3, 4, 5))
    first, last = r == 0, r == 7
    bit = (r ^ (2 * place[1])) & 2
    near_across, far_across = bit != 0, bit == 0

    def pair(q, _):
        diagonal = inverse_diagonal(lam, q, coef[HKD], coef[VALID])
        edge_diagonal = inverse_diagonal(lam, q, edge[1], edge[2])
        update = updater(lam, q, coef, diagonal)
        start = [[None] * FIELDS for _ in range(4)]
        edges = [[None] * FIELDS for _ in range(4)]
        for f in range(FIELDS):
            tiles = [[None, None] for _ in range(4)]
            far_tiles = [[None, None] for _ in range(4)]
            for c in range(2):
                for half in range(2):
                    centre = own[q, half, f, c]
                    a, b = across[q, half, f, c], inside[q, half, f, c]
                    near = jnp.where(near_across, a, b)
                    far = jnp.where(far_across, a, b)
                    for odd in range(2):
                        p = 2 * half + odd
                        inner, other = (6, 2) if odd else (2, 6)
                        tiles[p][c] = jnp.where(middle, roll(centre, inner), roll(near, other))
                        far_tiles[p][c] = roll(far, other)
            for p in range(4):
                start[p][f] = first_iterate(f, tiles[p], coef[A], diagonal)
                edges[p][f] = first_iterate(f, far_tiles[p], edge[0], edge_diagonal)
                for c in range(2):
                    x0[q, p, f, c] = start[p][f][c]
        none = [[0.0, 0.0]] * FIELDS
        for p in range(4):
            cur = plane(x0, q, p)
            up = plane(x0, q, p + 1) if p < 3 else none
            dn = plane(x0, q, p - 1) if p > 0 else none
            north = [[jnp.where(first, edges[p][f][c], cur[f][c]) for c in range(2)] for f in range(FIELDS)]
            south = [[jnp.where(last, edges[p][f][c], cur[f][c]) for c in range(2)] for f in range(FIELDS)]
            new = update(cur, up, dn, lambda f, c: 1.2 * cur[f][c], north, south)
            for f in range(FIELDS):
                for c in range(2):
                    x1[q, p, f, c] = new[f][c]
        return 0

    lax.fori_loop(0, PAIRS, pair, 0)


def solve_kernel(place, flags, lam, coef, even, odd, inside, across, start, second, out, xz, x1, x2, sol):
    r = rows()
    middle = among(r, (2, 3, 4, 5))
    upper = r < 4
    on_even = (r * 0 + place[0]) == 0
    core = r * 0 + place[1]
    pick_lo = (jnp.where(among(r, (3, 6, 7)), 1, 0) ^ core) == 1
    pick_hi = (jnp.where(among(r, (1, 4, 5)), 1, 0) ^ core) == 1

    def pair(q, _):
        m00, m11, m01 = lam[q, 0], lam[q, 1], lam[q, 2]
        diagonal = inverse_diagonal(lam, q, coef[HKD], coef[VALID])
        pa, pb, pc = diagonal
        update = updater(lam, q, coef, diagonal)
        for f in range(FIELDS):
            tiles = [[None, None] for _ in range(6)]
            for c in range(2):
                a, b = even[q, f, c], odd[q, f, c]
                lo, hi = jnp.where(on_even, b, a), jnp.where(on_even, a, b)
                a, b = across[q, f, c], inside[q, f, c]
                g1 = jnp.where(pick_lo, a, b)
                g2 = jnp.where(pick_hi, a, b)
                tiles[2][c] = jnp.where(middle, roll(lo, 6), roll(g1, 2))
                tiles[1][c] = jnp.where(middle, roll(lo, 2), roll(g1, 6))
                tiles[3][c] = jnp.where(middle, roll(hi, 2), roll(g2, 4))
                tiles[4][c] = jnp.where(middle, roll(hi, 6), g2)
            a, b = even[q, f, 2], odd[q, f, 2]
            lo, hi = jnp.where(on_even, b, a), jnp.where(on_even, a, b)
            tiles[0] = [roll(lo, 2), roll(lo, 6)]
            tiles[5] = [roll(hi, 2), roll(hi, 6)]
            for p in range(6):
                xz[p, f, 0], xz[p, f, 1] = first_iterate(f, tiles[p], coef[A], diagonal)

        def x0_at(p):
            if 0 <= p < 4:
                return plane(start, q, p)
            return plane(xz, p + 3 if p < 0 else p - 1)

        for p in (-2, -1, 4, 5):
            cur = x0_at(p)
            new = update(cur, x0_at(p + 1), x0_at(p - 1), lambda f, c: 1.2 * cur[f][c])
            keep = flags[0] if p < 0 else flags[1]
            for f in range(FIELDS):
                for c in range(2):
                    x1[p + 2, f, c] = keep * new[f][c]
        for p in (1, 2):
            for f in range(FIELDS):
                for c in range(2):
                    x1[p + 2, f, c] = second[q, p, f, c]
        for p, sign in ((0, -1.0), (3, 1.0)):
            side = x0_at(p + int(sign))
            for c in range(2):
                for f in range(3):
                    v = second[q, p, f, c] + coef[AC] * side[f][c]
                    if f == 2:
                        v = v - (sign * coef[G]) * side[3][c]
                    x1[p + 2, f, c] = v
            flow = [coef[KZ] * side[3][c] for c in range(2)]
            div = [(sign * 0.3) * side[2][c] for c in range(2)]
            g0 = flow[0] - (m00 * div[0] + m01 * div[1])
            g1 = flow[1] - (m11 * div[1] - m01 * div[0])
            x1[p + 2, 3, 0] = second[q, p, 3, 0] + pa * g0 + pc * g1
            x1[p + 2, 3, 1] = second[q, p, 3, 1] + pb * g1 - pc * g0

        for p in range(-1, 5):
            cur, base = plane(x1, p + 2), x0_at(p)
            new = update(cur, plane(x1, p + 3), plane(x1, p + 1), lambda f, c: base[f][c] + 0.2 * cur[f][c])
            for f in range(FIELDS):
                for c in range(2):
                    v = new[f][c]
                    if p < 0:
                        v = flags[0] * v
                    if p > 3:
                        v = flags[1] * v
                    x2[p + 1, f, c] = v
        for half in range(2):
            two = []
            for p in (2 * half, 2 * half + 1):
                cur, base = plane(x2, p + 1), x0_at(p)
                two.append(
                    update(cur, plane(x2, p + 2), plane(x2, p), lambda f, c: base[f][c] + 0.2 * cur[f][c])
                )
            for f in range(FIELDS):
                for c in range(2):
                    sol[q, half, f, c] = jnp.where(upper, roll(two[0][f][c], 6), roll(two[1][f][c], 2))
        return 0

    lax.fori_loop(0, PAIRS, pair, 0)

    scale32 = np.float32(1.0 / STEPS)

    def back(f, _):
        for half in range(2):
            tiles = [
                (sol[q, half, f, 0] * scale32, sol[q, half, f, 1] * scale32) for q in range(PAIRS)
            ]
            spec = [(tiles[0][0], None)] + tiles[1:] + [(tiles[0][1], None)]
            for t, v in enumerate(irfft(spec)):
                out[(t // 2) * 2 + half, f, t % 2] = v
        return 0

    lax.fori_loop(0, FIELDS, back, 0)


def call(kernel, outs, in_spaces, scratch=(), limit=4, micros=1):
    f32 = jnp.float32
    shapes = [jax.ShapeDtypeStruct(s, f32) for s in outs]
    specs = [pl.BlockSpec(memory_space=pltpu.VMEM) for _ in outs]
    single = len(outs) == 1
    return pl.pallas_call(
        kernel,
        out_shape=shapes[0] if single else shapes,
        in_specs=[pl.BlockSpec(memory_space=m) for m in in_spaces],
        out_specs=specs[0] if single else specs,
        scratch_shapes=[pltpu.VMEM(s, f32) for s in scratch],
        compiler_params=pltpu.CompilerParams(vmem_limit_bytes=limit * MIB),
        cost_estimate=pl.CostEstimate(flops=0, bytes_accessed=int(micros * 3.69e6), transcendentals=0),
    )


def lam_table():
    k = np.arange(1, PAIRS)
    real, imag = 1 - np.cos(2 * np.pi * k / STEPS), np.sin(2 * np.pi * k / STEPS)
    rest = np.stack([real, real, -imag], axis=1)
    return np.concatenate([[[0.0, 2.0, 0.0]], rest]).astype(np.float32)


def on_device(sources, regions, material):
    vmem, smem = pltpu.VMEM, pltpu.SMEM
    x = lax.axis_index("xh") * 2 + lax.axis_index("xl")
    y = lax.axis_index("y")
    z = lax.axis_index("z")
    pos = y * 4 + jnp.where(y % 2 == 1, 3 - x, x)
    block = 2 * pos + lax.axis_index("c")
    piece = (32, FIELDS, 2, 8, 128)

    def level(v):
        return lax.all_to_all(v, LEVEL, 0, 0, tiled=True)

    def swap(v, pairs):
        return lax.ppermute(v, AXES, pairs)

    arrived = level(call(split_kernel, [piece], [vmem])(sources))
    first_row = 4 * block
    wide = jnp.concatenate([regions[:8], regions, regions[:8]], axis=0)
    near = lax.dynamic_slice_in_dim(wide, first_row + 4, 16, axis=0)
    coef, edge = call(coefficient_kernel, [(16, 8, 128), (3, 8, 128)], [smem, smem, vmem])(
        first_row.astype(jnp.int32).reshape(1), material, near
    )
    place = jnp.stack([z % 2, lax.axis_index("c")]).astype(jnp.int32)
    flags = jnp.stack([(z > 0), (z < 7)]).astype(jnp.float32)
    arrived, coef, edge, place, flags = lax.optimization_barrier((arrived, coef, edge, place, flags))
    lam = jnp.asarray(lam_table())
    own, even, odd = call(
        spectrum_kernel,
        [(PAIRS, 2, FIELDS, 2, 8, 128)] + [(PAIRS, FIELDS, 3, 8, 128)] * 2,
        [smem, vmem],
        limit=8,
    )(place, arrived)
    even, odd = swap(even, level_swap(0)), swap(odd, level_swap(1))
    inside, across = swap(own, block_swap(0)), swap(own, block_swap(1))
    start, second = call(
        inner_kernel,
        [(PAIRS, 4, FIELDS, 2, 8, 128)] * 2,
        [smem, smem] + [vmem] * 5,
        limit=10,
        micros=5,
    )(place, lam, coef, edge, own, inside, across)
    corners = call(corner_kernel, [(PAIRS, FIELDS, 2, 8, 128)] * 2, [smem, vmem, vmem])(place, even, odd)
    inside, across = swap(corners[0], block_swap(0)), swap(corners[1], block_swap(1))
    answer = call(
        solve_kernel,
        [piece],
        [smem] * 3 + [vmem] * 7,
        scratch=[
            (6, FIELDS, 2, 8, 128),
            (8, FIELDS, 2, 8, 128),
            (6, FIELDS, 2, 8, 128),
            (PAIRS, 2, FIELDS, 2, 8, 128),
        ],
        limit=14,
    )(place, flags, lam, coef, even, odd, inside, across, start, second)
    return call(join_kernel, [(FIELDS, 2, 2, 128, 128)], [vmem])(level(answer))


def solution(mesh):
    fine = Mesh(mesh.devices.reshape([SIZES[a] for a in AXES]), AXES)
    spec = P(None, ("xl", "y", "c"), ("z", "xh"), None, None)
    return jax.shard_map(
        on_device, mesh=fine, in_specs=(spec, P(), P()), out_specs=spec, check_vma=False
    )
```

```python
import functools
import math

import jax
import jax.numpy as jnp
import numpy as np
from jax import lax
from jax.experimental import pallas as pl
from jax.experimental.pallas import tpu as pltpu
from jax.sharding import Mesh
from jax.sharding import PartitionSpec as P

AXES = ("xl", "y", "c", "z", "xh")
SIZES = dict(xl=2, y=4, c=2, z=8, xh=2)
LEVEL = ("xl", "y", "c", "xh")
STEPS = 32
PAIRS = 16
FIELDS = 4
MIB = 1 << 20
UNROLL = 4


def chip_at(pos):
    y, x = divmod(pos, 4)
    return (3 - x if y % 2 else x), y


def level_index(pos, core):
    x, y = chip_at(pos)
    return ((((x % 2) * 4 + y) * 2 + core) * 2) + x // 2


def device_index(z, pos, core):
    x, y = chip_at(pos)
    return ((((x % 2) * 4 + y) * 2 + core) * 8 + z) * 2 + x // 2


def both(pairs):
    return pairs + [(t, s) for s, t in pairs]


def sibling_swap():
    return both([(device_index(z, p, 0), device_index(z, p, 1)) for z in range(8) for p in range(16)])


def level_swap():
    return both([(device_index(z, p, 1), device_index(z + 1, p, 0)) for z in range(7) for p in range(16)])


def row_swap(parity):
    low = [p for p in range(15) if p % 2 == parity]
    return both([(device_index(z, p, c), device_index(z, p + 1, c)) for z in range(8) for p in low for c in range(2)])


def rows():
    return lax.broadcasted_iota(jnp.int32, (8, 128), 0)


def lanes():
    return lax.broadcasted_iota(jnp.int32, (8, 128), 1)


def among(index, members):
    mask = index == members[0]
    for member in members[1:]:
        mask = mask | (index == member)
    return mask


def roll(tile, amount):
    amount %= 8
    return tile if amount == 0 else pltpu.roll(tile, amount, 0)


def mul_const(re, im, cr, ci):
    def axpy(a, x, b, y):
        terms = []
        for k, v in ((a, x), (b, y)):
            if abs(k) > 1e-12:
                terms.append((k, v))
        total = None
        for k, v in terms:
            if total is None:
                total = v if abs(k - 1) < 1e-12 else (-v if abs(k + 1) < 1e-12 else v * np.float32(k))
            elif abs(k - 1) < 1e-12:
                total = total + v
            elif abs(k + 1) < 1e-12:
                total = total - v
            else:
                total = total + v * np.float32(k)
        return total

    if abs(abs(cr) - abs(ci)) < 1e-12:
        root = np.float32(abs(cr))
        sr, si = math.copysign(1, cr), math.copysign(1, ci)
        return axpy(sr, re * root, -si, im * root), axpy(si, re * root, sr, im * root)
    return axpy(cr, re, -ci, im), axpy(ci, re, cr, im)


def rfft(x):
    n = len(x)
    if n == 2:
        return [(x[0] + x[1], None), (x[0] - x[1], None)]
    even, odd = rfft(x[0::2]), rfft(x[1::2])
    out = [None] * (n // 2 + 1)
    out[0] = (even[0][0] + odd[0][0], None)
    out[n // 2] = (even[0][0] - odd[0][0], None)
    out[n // 4] = (even[n // 4][0], -odd[n // 4][0])
    for k in range(1, n // 4):
        angle = -2 * math.pi * k / n
        tr, ti = mul_const(*odd[k], math.cos(angle), math.sin(angle))
        er, ei = even[k]
        out[k] = (er + tr, ei + ti)
        out[n // 2 - k] = (er - tr, ti - ei)
    return out


def irfft(spec):
    n = 2 * (len(spec) - 1)
    if n == 2:
        return [spec[0][0] + spec[1][0], spec[0][0] - spec[1][0]]
    q = n // 4
    even, odd = [None] * (q + 1), [None] * (q + 1)
    even[0] = (spec[0][0] + spec[2 * q][0], None)
    odd[0] = (spec[0][0] - spec[2 * q][0], None)
    even[q] = (2.0 * spec[q][0], None)
    odd[q] = (-2.0 * spec[q][1], None)
    for k in range(1, q):
        ar, ai = spec[k]
        br, bi = spec[2 * q - k]
        even[k] = (ar + br, ai - bi)
        angle = 2 * math.pi * k / n
        odd[k] = mul_const(ar - br, ai + bi, math.cos(angle), math.sin(angle))
    a, b = irfft(even), irfft(odd)
    return [v for two in zip(a, b) for v in two]


def split_kernel(src, out, whole, pieces, in_sems, out_sems):
    arrivals = [pltpu.make_async_copy(src.at[f], whole.at[f], in_sems.at[f]) for f in range(FIELDS)]
    for copy in arrivals:
        copy.start()
    leaving = []
    for f in range(FIELDS):
        arrivals[f].wait()
        for t in range(2):
            for core in range(2):
                for pos in range(16):
                    pieces[level_index(pos, core), f, t] = whole[f, t, core, pl.ds(8 * pos, 8), :]
        leaving.append(pltpu.make_async_copy(pieces.at[:, f], out.at[:, f], out_sems.at[f]))
        leaving[-1].start()
    for copy in leaving:
        copy.wait()


def join_kernel(src, out, whole, sems):
    copies = []
    for f in range(FIELDS):
        for t in range(2):
            for core in range(2):
                for pos in range(16):
                    whole[f, t, core, pl.ds(8 * pos, 8), :] = src[level_index(pos, core), f, t]
        copies.append(pltpu.make_async_copy(whole.at[f], out.at[f], sems.at[f]))
        copies[-1].start()
    for copy in copies:
        copy.wait()


(A, AE, AW, AN, AS, AH, AC, GE, GW, GN, GS, GH, G, KE, KW, KN, KS, KH, KZ, HKD, DN, DS, DH) = range(23)


def coefficient_kernel(place, material, regions, coef):
    pos = place[1]
    r, l = rows(), lanes()
    there = [l < 127, l > 0, (r < 7) | (pos < 15), (r > 0) | (pos > 0)]
    has_e, has_w = [jnp.where(t, 1.0, 0.0).astype(jnp.float32) for t in there[:2]]
    here = regions[pl.ds(8 * pos, 8), :]
    after = regions[pl.ds(8 * jnp.minimum(pos + 1, 15), 8), :]
    before = regions[pl.ds(8 * jnp.maximum(pos - 1, 0), 8), :]

    def parts(row):
        def value_of(classes):
            value = jnp.zeros((8, 128), jnp.float32)
            for m in range(4):
                value = jnp.where(classes == m, material[row, m], value)
            return value

        value = value_of(here)
        moved = [
            pltpu.roll(value, 127, 1),
            pltpu.roll(value, 1, 1),
            roll(jnp.where(r == 0, value_of(after), value), 7),
            roll(jnp.where(r == 7, value_of(before), value), 1),
        ]
        return value, [jnp.where(t, (value + v) * 0.5, value) for t, v in zip(there, moved)]

    shear, (se, sw, sn, ss) = parts(0)
    _, (ke, kw, kn, ks) = parts(1)
    axial, _ = parts(2)
    a = 0.8 / (se + sw + sn + ss + 2.0 * shear)
    in_n, in_s = [jnp.where(t, 1.0, 0.0).astype(jnp.float32) for t in (r < 7, r > 0)]
    zero = jnp.zeros((8, 128), jnp.float32)

    def beside(south, north):
        return jnp.where(r == 0, south, jnp.where(r == 7, north, zero))

    g = 0.3 * a
    table = [
        a, a * se * has_e, a * sw * has_w, a * sn * in_n, a * ss * in_s, beside(a * ss, a * sn), a * shear,
        g * has_e, g * has_w, g * in_n, g * in_s, beside(-g, g), g,
        0.5 * ke * has_e, 0.5 * kw * has_w, 0.5 * kn * in_n, 0.5 * ks * in_s, beside(0.5 * ks, 0.5 * kn),
        0.5 * axial, 0.5 * (ke + kw + kn + ks + 2.0 * axial),
        0.3 * in_n, 0.3 * in_s, beside(zero - 0.3, zero + 0.3),
    ]
    for n, v in enumerate(table):
        coef[n] = v


def inverse_diagonal(lam, q, half_diag):
    d0, d1, di = half_diag + 0.5 * lam[q, 0], half_diag + 0.5 * lam[q, 1], -0.5 * lam[q, 2]
    inv = 0.8 / (d0 * d1 + di * di)
    return inv * d1, inv * d0, inv * di


def first_iterate(f, tiles, a, diagonal):
    re, im = tiles
    if f < 3:
        return a * re, a * im
    b00, b11, b01 = diagonal
    return b00 * re + b01 * im, b11 * im - b01 * re


def send(place, q, planes, row_a, row_b):
    r = rows()
    even = (r * 0 + place[1] % 2) == 0
    for p, tiles in planes:
        after = before = None
        for j in range(8):
            f, c = divmod(j, 2)
            seven, zero = roll(tiles[f][c], j + 1), roll(tiles[f][c], j - 1)
            after = seven if j == 0 else jnp.where(r == j, seven, after)
            before = zero if j == 0 else jnp.where(r == (j - 1) % 8, zero, before)
        row_a[q, p] = jnp.where(even, after, before)
        row_b[q, p] = jnp.where(even, before, after)


def spectrum_kernel(place, lam, coef, src, x0, outer, row_a, row_b, spec):
    def body(f, _):
        for p in range(2):
            got = rfft([src[(t // 2) * 2 + p, f, t % 2] for t in range(STEPS)])
            pairs = [(got[0][0], got[16][0])] + got[1:16]
            for q in range(PAIRS):
                for c in range(2):
                    spec[q, p, f, c] = pairs[q][c]
        return 0

    lax.fori_loop(0, FIELDS, body, 0)

    def pair(q, _):
        diagonal = inverse_diagonal(lam, q, coef[HKD])
        planes = [
            [first_iterate(f, (spec[q, p, f, 0], spec[q, p, f, 1]), coef[A], diagonal) for f in range(FIELDS)]
            for p in range(2)
        ]
        for p in range(2):
            for f in range(FIELDS):
                for c in range(2):
                    x0[q, p, f, c] = planes[p][f][c]
        for f in range(FIELDS):
            for c in range(2):
                outer[q, f, c] = x0[q, place[0], f, c]
        send(place, q, list(enumerate(planes)), row_a, row_b)
        return 0

    lax.fori_loop(0, PAIRS, pair, 0, unroll=UNROLL)


def own_kernel(place, lam, coef, x0, x, sib, part):
    l = lanes()
    east = jnp.where(l == 127, 0.0, 0.3).astype(jnp.float32)
    west = jnp.where(l == 0, 0.0, 0.3).astype(jnp.float32)
    core = place[0]
    sign = 1.0 - 2.0 * core.astype(jnp.float32)

    def pair(q, _):
        m00, m11, m01 = lam[q, 0], lam[q, 1], lam[q, 2]
        pa, pb, pc = inverse_diagonal(lam, q, coef[HKD])
        for p, edge in ((core, True), (1 - core, False)):
            new = [[None, None] for _ in range(FIELDS)]
            div, flow = [None, None], [None, None]
            for c in range(2):
                cur = [x[q, p, f, c] for f in range(FIELDS)]
                es = [pltpu.roll(v, 127, 1) for v in cur]
                ws = [pltpu.roll(v, 1, 1) for v in cur]
                ns = [roll(v, 7) for v in cur]
                ss = [roll(v, 1) for v in cur]
                if edge:
                    total = [sib[q, core, f, c] for f in range(FIELDS)]
                    drop_u, drop_p = sign * total[2], sign * total[3]
                else:
                    dn = [sib[q, 0, f, c] for f in range(FIELDS)]
                    up = [sib[q, 1, f, c] for f in range(FIELDS)]
                    total = [u + d for u, d in zip(up, dn)]
                    drop_u, drop_p = up[2] - dn[2], up[3] - dn[3]
                grad = [
                    coef[GE] * es[3] - coef[GW] * ws[3],
                    coef[GN] * ns[3] - coef[GS] * ss[3],
                    coef[G] * drop_p,
                ]
                for f in range(3):
                    v = (x0[q, p, f, c] + 0.2 * cur[f]) + coef[AE] * es[f] + coef[AW] * ws[f]
                    v = v + coef[AN] * ns[f] + coef[AS] * ss[f]
                    part[q, p, f, c] = v + coef[AC] * total[f] - grad[f]
                new[3][c] = x0[q, p, 3, c] + 0.2 * cur[3]
                flow[c] = (
                    coef[KE] * es[3]
                    + coef[KW] * ws[3]
                    + coef[KN] * ns[3]
                    + coef[KS] * ss[3]
                    + coef[KZ] * total[3]
                )
                div[c] = east * es[0] - west * ws[0] + coef[DN] * ns[1] - coef[DS] * ss[1] + 0.3 * drop_u
            g0 = flow[0] - (m00 * div[0] + m01 * div[1])
            g1 = flow[1] - (m11 * div[1] - m01 * div[0])
            part[q, p, 3, 0] = new[3][0] + pa * g0 + pc * g1
            part[q, p, 3, 1] = new[3][1] + pb * g1 - pc * g0
        return 0

    lax.fori_loop(0, PAIRS, pair, 0, unroll=UNROLL)


def finish(place, lam, q, coef, part, outer, row_a, row_b):
    r = rows()
    core = place[0]
    sign = 2.0 * core.astype(jnp.float32) - 1.0
    odd = r * 0 + place[1] % 2
    m00, m11, m01 = lam[q, 0], lam[q, 1], lam[q, 2]
    pa, pb, pc = inverse_diagonal(lam, q, coef[HKD])
    result = []
    for p, edge in ((core, True), (1 - core, False)):
        a, b = row_a[q, p], row_b[q, p]
        new = [[None, None] for _ in range(FIELDS)]
        div, flow = [None, None], [None, None]
        for c in range(2):
            beside = []
            for f in range(FIELDS):
                j = 2 * f + c
                low_is_b = (jnp.where(r == j, 1, 0) ^ odd) == 1
                beside.append(roll(jnp.where(low_is_b, b, a), -j))
            for f in range(3):
                new[f][c] = part[q, p, f, c] + coef[AH] * beside[f]
            new[1][c] = new[1][c] - coef[GH] * beside[3]
            flow[c] = coef[KH] * beside[3]
            div[c] = coef[DH] * beside[1]
            if edge:
                out = [outer[q, f, c] for f in range(FIELDS)]
                for f in range(3):
                    new[f][c] = new[f][c] + coef[AC] * out[f]
                new[2][c] = new[2][c] - (sign * coef[G]) * out[3]
                flow[c] = flow[c] + coef[KZ] * out[3]
                div[c] = div[c] + (0.3 * sign) * out[2]
        g0 = flow[0] - (m00 * div[0] + m01 * div[1])
        g1 = flow[1] - (m11 * div[1] - m01 * div[0])
        new[3][0] = part[q, p, 3, 0] + pa * g0 + pc * g1
        new[3][1] = part[q, p, 3, 1] + pb * g1 - pc * g0
        result.append((p, new))
    return result


def round_kernel(place, lam, coef, part, outer, row_a, row_b, y, next_outer, next_a, next_b):
    def pair(q, _):
        planes = finish(place, lam, q, coef, part, outer, row_a, row_b)
        for p, tiles in planes:
            for f in range(FIELDS):
                for c in range(2):
                    y[q, p, f, c] = tiles[f][c]
        for f in range(FIELDS):
            for c in range(2):
                next_outer[q, f, c] = planes[0][1][f][c]
        send(place, q, planes, next_a, next_b)
        return 0

    lax.fori_loop(0, PAIRS, pair, 0, unroll=UNROLL)


def last_kernel(place, lam, coef, part, outer, row_a, row_b, out, y):
    scale32 = np.float32(1.0 / STEPS)

    def pair(q, _):
        for p, tiles in finish(place, lam, q, coef, part, outer, row_a, row_b):
            for f in range(FIELDS):
                for c in range(2):
                    y[q, p, f, c] = tiles[f][c] * scale32
        return 0

    lax.fori_loop(0, PAIRS, pair, 0, unroll=UNROLL)

    def back(f, _):
        for p in range(2):
            spec = [(y[0, p, f, 0], None)]
            spec += [(y[q, p, f, 0], y[q, p, f, 1]) for q in range(1, PAIRS)]
            spec += [(y[0, p, f, 1], None)]
            for t, v in enumerate(irfft(spec)):
                out[(t // 2) * 2 + p, f, t % 2] = v
        return 0

    lax.fori_loop(0, FIELDS, back, 0)


def call(kernel, outs, in_spaces, scratch=(), limit=4, micros=1):
    f32 = jnp.float32
    shapes = [jax.ShapeDtypeStruct(s, f32) for s in outs]
    specs = [pl.BlockSpec(memory_space=pltpu.VMEM) for _ in outs]
    single = len(outs) == 1
    return pl.pallas_call(
        kernel,
        out_shape=shapes[0] if single else shapes,
        in_specs=[pl.BlockSpec(memory_space=m) for m in in_spaces],
        out_specs=specs[0] if single else specs,
        scratch_shapes=[pltpu.VMEM(s, f32) for s in scratch],
        compiler_params=pltpu.CompilerParams(vmem_limit_bytes=limit * MIB),
        cost_estimate=pl.CostEstimate(flops=0, bytes_accessed=int(micros * 3.69e6), transcendentals=0),
    )


def lam_table():
    k = np.arange(1, PAIRS)
    real, imag = 1 - np.cos(2 * np.pi * k / STEPS), np.sin(2 * np.pi * k / STEPS)
    rest = np.stack([real, real, -imag], axis=1)
    return np.concatenate([[[0.0, 2.0, 0.0]], rest]).astype(np.float32)


def on_device(sources, regions, material):
    vmem, smem = pltpu.VMEM, pltpu.SMEM
    x = lax.axis_index("xh") * 2 + lax.axis_index("xl")
    y = lax.axis_index("y")
    pos = y * 4 + jnp.where(y % 2 == 1, 3 - x, x)
    place = jnp.stack([lax.axis_index("c"), pos]).astype(jnp.int32)
    piece = (32, FIELDS, 2, 8, 128)
    block = (PAIRS, 2, FIELDS, 2, 8, 128)
    messages = [(PAIRS, FIELDS, 2, 8, 128), (PAIRS, 2, 8, 128), (PAIRS, 2, 8, 128)]

    def level(v):
        return lax.all_to_all(v, LEVEL, 0, 0, tiled=True)

    def exchange(v, outer, row_a, row_b):
        outer = lax.ppermute(outer, AXES, level_swap())
        sib = lax.ppermute(v, AXES, sibling_swap())
        row_a = lax.ppermute(row_a, AXES, row_swap(0))
        row_b = lax.ppermute(row_b, AXES, row_swap(1))
        part = call(own_kernel, [block], [smem, smem] + [vmem] * 4, limit=8, micros=2)(place, lam, coef, x0, v, sib)
        return part, outer, row_a, row_b

    whole = (FIELDS, 2, 2, 128, 128)
    pieces = pl.pallas_call(
        split_kernel,
        out_shape=jax.ShapeDtypeStruct(piece, jnp.float32),
        in_specs=[pl.BlockSpec(memory_space=pltpu.HBM)],
        out_specs=pl.BlockSpec(memory_space=pltpu.HBM),
        scratch_shapes=[
            pltpu.VMEM(whole, jnp.float32),
            pltpu.VMEM(piece, jnp.float32),
            pltpu.SemaphoreType.DMA((FIELDS,)),
            pltpu.SemaphoreType.DMA((FIELDS,)),
        ],
        compiler_params=pltpu.CompilerParams(vmem_limit_bytes=60 * MIB),
    )(sources)
    arrived = level(pieces)
    coef = call(coefficient_kernel, [(23, 8, 128)], [smem, smem, vmem])(place, material, regions)
    arrived, coef, place = lax.optimization_barrier((arrived, coef, place))
    lam = jnp.asarray(lam_table())
    x0, *out = call(spectrum_kernel, [block] + messages, [smem, smem, vmem, vmem], [block], 8)(
        place, lam, coef, arrived
    )
    x = x0
    for _ in range(2):
        x, *out = call(round_kernel, [block] + messages, [smem, smem] + [vmem] * 5, limit=8)(
            place, lam, coef, *exchange(x, *out)
        )
    answer = call(last_kernel, [piece], [smem, smem] + [vmem] * 5, [block], 8)(
        place, lam, coef, *exchange(x, *out)
    )
    return pl.pallas_call(
        join_kernel,
        out_shape=jax.ShapeDtypeStruct(whole, jnp.float32),
        in_specs=[pl.BlockSpec(memory_space=vmem)],
        out_specs=pl.BlockSpec(memory_space=pltpu.HBM),
        scratch_shapes=[pltpu.VMEM(whole, jnp.float32), pltpu.SemaphoreType.DMA((FIELDS,))],
        compiler_params=pltpu.CompilerParams(vmem_limit_bytes=4 * MIB),
    )(level(answer))


def solution(mesh):
    fine = Mesh(mesh.devices.reshape([SIZES[a] for a in AXES]), AXES)
    spec = P(None, ("xl", "y", "c"), ("z", "xh"), None, None)
    return jax.shard_map(
        on_device, mesh=fine, in_specs=(spec, P(), P()), out_specs=spec, check_vma=False
    )
```

```python
import functools
import math

import jax
import jax.numpy as jnp
import numpy as np
from jax import lax
from jax.experimental import pallas as pl
from jax.experimental.pallas import tpu as pltpu
from jax.sharding import Mesh
from jax.sharding import PartitionSpec as P

AXES = ("xl", "y", "c", "z", "xh")
SIZES = dict(xl=2, y=4, c=2, z=8, xh=2)
LEVEL = ("xl", "y", "c", "xh")
STEPS = 32
PAIRS = 16
FIELDS = 4
MIB = 1 << 20
UNROLL = 4


def chip_at(pos):
    y, x = divmod(pos, 4)
    return (3 - x if y % 2 else x), y


def level_index(pos, core):
    x, y = chip_at(pos)
    return ((((x % 2) * 4 + y) * 2 + core) * 2) + x // 2


def device_index(z, pos, core):
    x, y = chip_at(pos)
    return ((((x % 2) * 4 + y) * 2 + core) * 8 + z) * 2 + x // 2


def both(pairs):
    return pairs + [(t, s) for s, t in pairs]


def sibling_swap():
    return both([(device_index(z, p, 0), device_index(z, p, 1)) for z in range(8) for p in range(16)])


def level_swap():
    return both([(device_index(z, p, 1), device_index(z + 1, p, 0)) for z in range(7) for p in range(16)])


def row_swap(parity):
    low = [p for p in range(15) if p % 2 == parity]
    return both([(device_index(z, p, c), device_index(z, p + 1, c)) for z in range(8) for p in low for c in range(2)])


def core_index():
    return lax.axis_index("c")


def row_block():
    x, y = lax.axis_index("xh") * 2 + lax.axis_index("xl"), lax.axis_index("y")
    return y * 4 + jnp.where(y % 2 == 1, 3 - x, x)


def rows():
    return lax.broadcasted_iota(jnp.int32, (8, 128), 0)


def lanes():
    return lax.broadcasted_iota(jnp.int32, (8, 128), 1)


def among(index, members):
    mask = index == members[0]
    for member in members[1:]:
        mask = mask | (index == member)
    return mask


def roll(tile, amount):
    amount %= 8
    return tile if amount == 0 else pltpu.roll(tile, amount, 0)


def mul_const(re, im, cr, ci):
    def axpy(a, x, b, y):
        terms = []
        for k, v in ((a, x), (b, y)):
            if abs(k) > 1e-12:
                terms.append((k, v))
        total = None
        for k, v in terms:
            if total is None:
                total = v if abs(k - 1) < 1e-12 else (-v if abs(k + 1) < 1e-12 else v * np.float32(k))
            elif abs(k - 1) < 1e-12:
                total = total + v
            elif abs(k + 1) < 1e-12:
                total = total - v
            else:
                total = total + v * np.float32(k)
        return total

    if abs(abs(cr) - abs(ci)) < 1e-12:
        root = np.float32(abs(cr))
        sr, si = math.copysign(1, cr), math.copysign(1, ci)
        return axpy(sr, re * root, -si, im * root), axpy(si, re * root, sr, im * root)
    return axpy(cr, re, -ci, im), axpy(ci, re, cr, im)


def rfft(x):
    n = len(x)
    if n == 2:
        return [(x[0] + x[1], None), (x[0] - x[1], None)]
    even, odd = rfft(x[0::2]), rfft(x[1::2])
    out = [None] * (n // 2 + 1)
    out[0] = (even[0][0] + odd[0][0], None)
    out[n // 2] = (even[0][0] - odd[0][0], None)
    out[n // 4] = (even[n // 4][0], -odd[n // 4][0])
    for k in range(1, n // 4):
        angle = -2 * math.pi * k / n
        tr, ti = mul_const(*odd[k], math.cos(angle), math.sin(angle))
        er, ei = even[k]
        out[k] = (er + tr, ei + ti)
        out[n // 2 - k] = (er - tr, ti - ei)
    return out


def irfft(spec):
    n = 2 * (len(spec) - 1)
    if n == 2:
        return [spec[0][0] + spec[1][0], spec[0][0] - spec[1][0]]
    q = n // 4
    even, odd = [None] * (q + 1), [None] * (q + 1)
    even[0] = (spec[0][0] + spec[2 * q][0], None)
    odd[0] = (spec[0][0] - spec[2 * q][0], None)
    even[q] = (2.0 * spec[q][0], None)
    odd[q] = (-2.0 * spec[q][1], None)
    for k in range(1, q):
        ar, ai = spec[k]
        br, bi = spec[2 * q - k]
        even[k] = (ar + br, ai - bi)
        angle = 2 * math.pi * k / n
        odd[k] = mul_const(ar - br, ai + bi, math.cos(angle), math.sin(angle))
    a, b = irfft(even), irfft(odd)
    return [v for two in zip(a, b) for v in two]


def split_kernel(src, out, whole, pieces, in_sems, out_sems):
    arrivals = [pltpu.make_async_copy(src.at[f], whole.at[f], in_sems.at[f]) for f in range(FIELDS)]
    for copy in arrivals:
        copy.start()
    leaving = []
    for f in range(FIELDS):
        arrivals[f].wait()
        for t in range(2):
            for core in range(2):
                for pos in range(16):
                    pieces[level_index(pos, core), f, t] = whole[f, t, core, pl.ds(8 * pos, 8), :]
        leaving.append(pltpu.make_async_copy(pieces.at[:, f], out.at[:, f], out_sems.at[f]))
        leaving[-1].start()
    for copy in leaving:
        copy.wait()


def join_kernel(src, out, whole, sems):
    copies = []
    for f in range(FIELDS):
        for t in range(2):
            for core in range(2):
                for pos in range(16):
                    whole[f, t, core, pl.ds(8 * pos, 8), :] = src[level_index(pos, core), f, t]
        copies.append(pltpu.make_async_copy(whole.at[f], out.at[f], sems.at[f]))
        copies[-1].start()
    for copy in copies:
        copy.wait()


(A, AE, AW, AN, AS, AH, AC, GE, GW, GN, GS, GH, G, KE, KW, KN, KS, KH, KZ, DN, DS, DH) = range(22)


def coefficient_kernel(material, regions, coef, table):
    pos = row_block()
    r, l = rows(), lanes()
    there = [l < 127, l > 0, (r < 7) | (pos < 15), (r > 0) | (pos > 0)]
    has_e, has_w = [jnp.where(t, 1.0, 0.0).astype(jnp.float32) for t in there[:2]]
    here = regions[pl.ds(8 * pos, 8), :]
    after = regions[pl.ds(8 * jnp.minimum(pos + 1, 15), 8), :]
    before = regions[pl.ds(8 * jnp.maximum(pos - 1, 0), 8), :]

    def parts(row):
        def value_of(classes):
            value = jnp.zeros((8, 128), jnp.float32)
            for m in range(4):
                value = jnp.where(classes == m, material[row, m], value)
            return value

        value = value_of(here)
        moved = [
            pltpu.roll(value, 127, 1),
            pltpu.roll(value, 1, 1),
            roll(jnp.where(r == 0, value_of(after), value), 7),
            roll(jnp.where(r == 7, value_of(before), value), 1),
        ]
        return value, [jnp.where(t, (value + v) * 0.5, value) for t, v in zip(there, moved)]

    shear, (se, sw, sn, ss) = parts(0)
    _, (ke, kw, kn, ks) = parts(1)
    axial, _ = parts(2)
    a = 0.8 / (se + sw + sn + ss + 2.0 * shear)
    in_n, in_s = [jnp.where(t, 1.0, 0.0).astype(jnp.float32) for t in (r < 7, r > 0)]
    zero = jnp.zeros((8, 128), jnp.float32)

    def beside(south, north):
        return jnp.where(r == 0, south, jnp.where(r == 7, north, zero))

    g = 0.3 * a
    half_diag = 0.5 * (ke + kw + kn + ks + 2.0 * axial)
    tiles = [
        a, a * se * has_e, a * sw * has_w, a * sn * in_n, a * ss * in_s, beside(a * ss, a * sn), a * shear,
        g * has_e, g * has_w, g * in_n, g * in_s, beside(-g, g), g,
        0.5 * ke * has_e, 0.5 * kw * has_w, 0.5 * kn * in_n, 0.5 * ks * in_s, beside(0.5 * ks, 0.5 * kn),
        0.5 * axial,
        0.3 * in_n, 0.3 * in_s, beside(zero - 0.3, zero + 0.3),
    ]
    for n, v in enumerate(tiles):
        coef[n] = v
    for q in range(PAIRS):
        m00, m11, m01 = 0.0, 2.0, 0.0
        if q:
            angle = 2 * math.pi * q / STEPS
            m00 = m11 = 1 - math.cos(angle)
            m01 = -math.sin(angle)
        d0, d1, di = half_diag + 0.5 * m00, half_diag + 0.5 * m11, -0.5 * m01
        inv = 0.8 / (d0 * d1 + di * di)
        for n, v in enumerate((zero + m00, zero + m11, zero + m01, inv * d1, inv * d0, inv * di)):
            table[q, n] = v


def first_iterate(f, tiles, a, diagonal):
    re, im = tiles
    if f < 3:
        return a * re, a * im
    b00, b11, b01 = diagonal
    return b00 * re + b01 * im, b11 * im - b01 * re


TALL = 8 * 2 * FIELDS


def tile(j):
    return pl.ds(8 * j, 8)


def every(row):
    return pl.ds(row, 8, stride=8)


def send(q, block, row_a, row_b):
    even = (rows() * 0 + row_block() % 2) == 0
    for p in range(2):
        after, before = block[q, p, every(7), :], block[q, p, every(0), :]
        row_a[q, p] = jnp.where(even, after, before)
        row_b[q, p] = jnp.where(even, before, after)


def spectrum_kernel(coef, table, src, x0, outer, row_a, row_b, spec):
    def body(f, _):
        for p in range(2):
            got = rfft([src[(t // 2) * 2 + p, f, t % 2] for t in range(STEPS)])
            pairs = [(got[0][0], got[16][0])] + got[1:16]
            for q in range(PAIRS):
                for c in range(2):
                    spec[q, p, f, c] = pairs[q][c]
        return 0

    lax.fori_loop(0, FIELDS, body, 0)

    def pair(q, _):
        diagonal = table[q, 3], table[q, 4], table[q, 5]
        for p in range(2):
            for f in range(FIELDS):
                got = first_iterate(f, (spec[q, p, f, 0], spec[q, p, f, 1]), coef[A], diagonal)
                for c in range(2):
                    x0[q, p, tile(2 * f + c), :] = got[c]
        outer[q] = x0[q, core_index()]
        send(q, x0, row_a, row_b)
        return 0

    lax.fori_loop(0, PAIRS, pair, 0, unroll=UNROLL)


def own_kernel(coef, table, x0, x, sib, part):
    l = lanes()
    east = jnp.where(l == 127, 0.0, 0.3).astype(jnp.float32)
    west = jnp.where(l == 0, 0.0, 0.3).astype(jnp.float32)
    core = core_index()
    sign = 1.0 - 2.0 * core.astype(jnp.float32)

    def pair(q, _):
        m00, m11, m01 = table[q, 0], table[q, 1], table[q, 2]
        pa, pb, pc = table[q, 3], table[q, 4], table[q, 5]
        for p, edge in ((core, True), (1 - core, False)):
            new = [[None, None] for _ in range(FIELDS)]
            div, flow = [None, None], [None, None]
            for c in range(2):
                cur = [x[q, p, tile(2 * f + c), :] for f in range(FIELDS)]
                es = [pltpu.roll(v, 127, 1) for v in cur]
                ws = [pltpu.roll(v, 1, 1) for v in cur]
                ns = [roll(v, 7) for v in cur]
                ss = [roll(v, 1) for v in cur]
                if edge:
                    total = [sib[q, core, tile(2 * f + c), :] for f in range(FIELDS)]
                    drop_u, drop_p = sign * total[2], sign * total[3]
                else:
                    dn = [sib[q, 0, tile(2 * f + c), :] for f in range(FIELDS)]
                    up = [sib[q, 1, tile(2 * f + c), :] for f in range(FIELDS)]
                    total = [u + d for u, d in zip(up, dn)]
                    drop_u, drop_p = up[2] - dn[2], up[3] - dn[3]
                grad = [
                    coef[GE] * es[3] - coef[GW] * ws[3],
                    coef[GN] * ns[3] - coef[GS] * ss[3],
                    coef[G] * drop_p,
                ]
                for f in range(3):
                    v = (x0[q, p, tile(2 * f + c), :] + 0.2 * cur[f]) + coef[AE] * es[f] + coef[AW] * ws[f]
                    v = v + coef[AN] * ns[f] + coef[AS] * ss[f]
                    part[q, p, tile(2 * f + c), :] = v + coef[AC] * total[f] - grad[f]
                new[3][c] = x0[q, p, tile(6 + c), :] + 0.2 * cur[3]
                flow[c] = (
                    coef[KE] * es[3]
                    + coef[KW] * ws[3]
                    + coef[KN] * ns[3]
                    + coef[KS] * ss[3]
                    + coef[KZ] * total[3]
                )
                div[c] = east * es[0] - west * ws[0] + coef[DN] * ns[1] - coef[DS] * ss[1] + 0.3 * drop_u
            g0 = flow[0] - (m00 * div[0] + m01 * div[1])
            g1 = flow[1] - (m11 * div[1] - m01 * div[0])
            part[q, p, tile(6), :] = new[3][0] + pa * g0 + pc * g1
            part[q, p, tile(7), :] = new[3][1] + pb * g1 - pc * g0
        return 0

    lax.fori_loop(0, PAIRS, pair, 0, unroll=UNROLL)


def finish(q, coef, table, part, outer, row_a, row_b, edges):
    r = rows()
    core = core_index()
    sign = 2.0 * core.astype(jnp.float32) - 1.0
    even = (r * 0 + row_block() % 2) == 0
    m00, m11, m01 = table[q, 0], table[q, 1], table[q, 2]
    pa, pb, pc = table[q, 3], table[q, 4], table[q, 5]
    result = []
    for n, p, edge in ((0, core, True), (1, 1 - core, False)):
        a, b = row_a[q, p], row_b[q, p]
        edges[q % UNROLL, n, every(0), :] = jnp.where(even, b, a)
        edges[q % UNROLL, n, every(7), :] = jnp.where(even, a, b)
        new = [[None, None] for _ in range(FIELDS)]
        div, flow = [None, None], [None, None]
        for c in range(2):
            beside = [edges[q % UNROLL, n, tile(2 * f + c), :] for f in range(FIELDS)]
            for f in range(3):
                new[f][c] = part[q, p, tile(2 * f + c), :] + coef[AH] * beside[f]
            new[1][c] = new[1][c] - coef[GH] * beside[3]
            flow[c] = coef[KH] * beside[3]
            div[c] = coef[DH] * beside[1]
            if edge:
                out = [outer[q, tile(2 * f + c), :] for f in range(FIELDS)]
                for f in range(3):
                    new[f][c] = new[f][c] + coef[AC] * out[f]
                new[2][c] = new[2][c] - (sign * coef[G]) * out[3]
                flow[c] = flow[c] + coef[KZ] * out[3]
                div[c] = div[c] + (0.3 * sign) * out[2]
        g0 = flow[0] - (m00 * div[0] + m01 * div[1])
        g1 = flow[1] - (m11 * div[1] - m01 * div[0])
        new[3][0] = part[q, p, tile(6), :] + pa * g0 + pc * g1
        new[3][1] = part[q, p, tile(7), :] + pb * g1 - pc * g0
        result.append((p, new))
    return result


def clear(edges):
    edges[...] = jnp.zeros(edges.shape, jnp.float32)


def round_kernel(coef, table, part, outer, row_a, row_b, y, next_outer, next_a, next_b, edges):
    clear(edges)

    def pair(q, _):
        for p, tiles in finish(q, coef, table, part, outer, row_a, row_b, edges):
            for j in range(2 * FIELDS):
                y[q, p, tile(j), :] = tiles[j // 2][j % 2]
        next_outer[q] = y[q, core_index()]
        send(q, y, next_a, next_b)
        return 0

    lax.fori_loop(0, PAIRS, pair, 0, unroll=UNROLL)


def last_kernel(coef, table, part, outer, row_a, row_b, out, y, edges):
    clear(edges)
    scale32 = np.float32(1.0 / STEPS)

    def pair(q, _):
        for p, tiles in finish(q, coef, table, part, outer, row_a, row_b, edges):
            for j in range(2 * FIELDS):
                y[q, p, j // 2, j % 2] = tiles[j // 2][j % 2] * scale32
        return 0

    lax.fori_loop(0, PAIRS, pair, 0, unroll=UNROLL)

    def back(f, _):
        for p in range(2):
            spec = [(y[0, p, f, 0], None)]
            spec += [(y[q, p, f, 0], y[q, p, f, 1]) for q in range(1, PAIRS)]
            spec += [(y[0, p, f, 1], None)]
            for t, v in enumerate(irfft(spec)):
                out[(t // 2) * 2 + p, f, t % 2] = v
        return 0

    lax.fori_loop(0, FIELDS, back, 0)


def call(kernel, outs, in_spaces, scratch=(), limit=4, micros=1):
    f32 = jnp.float32
    shapes = [jax.ShapeDtypeStruct(s, f32) for s in outs]
    specs = [pl.BlockSpec(memory_space=pltpu.VMEM) for _ in outs]
    single = len(outs) == 1
    return pl.pallas_call(
        kernel,
        out_shape=shapes[0] if single else shapes,
        in_specs=[pl.BlockSpec(memory_space=m) for m in in_spaces],
        out_specs=specs[0] if single else specs,
        scratch_shapes=[pltpu.VMEM(s, f32) for s in scratch],
        compiler_params=pltpu.CompilerParams(vmem_limit_bytes=limit * MIB),
        cost_estimate=pl.CostEstimate(flops=0, bytes_accessed=int(micros * 3.69e6), transcendentals=0),
    )


def on_device(sources, regions, material):
    vmem, smem = pltpu.VMEM, pltpu.SMEM
    piece = (32, FIELDS, 2, 8, 128)
    block = (PAIRS, 2, TALL, 128)
    apart = (PAIRS, 2, FIELDS, 2, 8, 128)
    messages = [(PAIRS, TALL, 128), (PAIRS, 2, 8, 128), (PAIRS, 2, 8, 128)]
    edges = (UNROLL, 2, TALL, 128)

    def level(v):
        return lax.all_to_all(v, LEVEL, 0, 0, tiled=True)

    def exchange(v, outer, row_a, row_b):
        outer = lax.ppermute(outer, AXES, level_swap())
        sib = lax.ppermute(v, AXES, sibling_swap())
        row_a = lax.ppermute(row_a, AXES, row_swap(0))
        row_b = lax.ppermute(row_b, AXES, row_swap(1))
        part = call(own_kernel, [block], [vmem] * 5, limit=8, micros=2)(coef, table, x0, v, sib)
        return part, outer, row_a, row_b

    whole = (FIELDS, 2, 2, 128, 128)
    pieces = pl.pallas_call(
        split_kernel,
        out_shape=jax.ShapeDtypeStruct(piece, jnp.float32),
        in_specs=[pl.BlockSpec(memory_space=pltpu.HBM)],
        out_specs=pl.BlockSpec(memory_space=pltpu.HBM),
        scratch_shapes=[
            pltpu.VMEM(whole, jnp.float32),
            pltpu.VMEM(piece, jnp.float32),
            pltpu.SemaphoreType.DMA((FIELDS,)),
            pltpu.SemaphoreType.DMA((FIELDS,)),
        ],
        compiler_params=pltpu.CompilerParams(vmem_limit_bytes=60 * MIB),
    )(sources)
    arrived = level(pieces)
    coef, table = call(coefficient_kernel, [(22, 8, 128), (PAIRS, 6, 8, 128)], [smem, vmem])(material, regions)
    arrived, coef, table = lax.optimization_barrier((arrived, coef, table))
    x0, *out = call(spectrum_kernel, [block] + messages, [vmem] * 3, [apart], 8)(
        coef, table, arrived
    )
    x = x0
    for _ in range(2):
        x, *out = call(round_kernel, [block] + messages, [vmem] * 6, [edges], 8)(
            coef, table, *exchange(x, *out)
        )
    answer = call(last_kernel, [piece], [vmem] * 6, [apart, edges], 8)(
        coef, table, *exchange(x, *out)
    )
    return pl.pallas_call(
        join_kernel,
        out_shape=jax.ShapeDtypeStruct(whole, jnp.float32),
        in_specs=[pl.BlockSpec(memory_space=vmem)],
        out_specs=pl.BlockSpec(memory_space=pltpu.HBM),
        scratch_shapes=[pltpu.VMEM(whole, jnp.float32), pltpu.SemaphoreType.DMA((FIELDS,))],
        compiler_params=pltpu.CompilerParams(vmem_limit_bytes=4 * MIB),
    )(level(answer))


def solution(mesh):
    fine = Mesh(mesh.devices.reshape([SIZES[a] for a in AXES]), AXES)
    spec = P(None, ("xl", "y", "c"), ("z", "xh"), None, None)
    return jax.shard_map(
        on_device, mesh=fine, in_specs=(spec, P(), P()), out_specs=spec, check_vma=False
    )
```

```python
import functools
import math

import jax
import jax.numpy as jnp
import numpy as np
from jax import lax
from jax.experimental import pallas as pl
from jax.experimental.pallas import tpu as pltpu
from jax.sharding import Mesh
from jax.sharding import PartitionSpec as P

AXES = ("xl", "y", "c", "z", "xh")
SIZES = dict(xl=2, y=4, c=2, z=8, xh=2)
LEVEL = ("xl", "y", "c", "xh")
STEPS = 32
PAIRS = 16
FIELDS = 4
MIB = 1 << 20
UNROLL = 4


def chip_at(pos):
    y, x = divmod(pos, 4)
    return (3 - x if y % 2 else x), y


def level_index(pos, core):
    x, y = chip_at(pos)
    return ((((x % 2) * 4 + y) * 2 + core) * 2) + x // 2


def device_index(z, pos, core):
    x, y = chip_at(pos)
    return ((((x % 2) * 4 + y) * 2 + core) * 8 + z) * 2 + x // 2


def both(pairs):
    return pairs + [(t, s) for s, t in pairs]


def sibling_swap():
    return both([(device_index(z, p, 0), device_index(z, p, 1)) for z in range(8) for p in range(16)])


def level_swap():
    return both([(device_index(z, p, 1), device_index(z + 1, p, 0)) for z in range(7) for p in range(16)])


def row_swap(parity):
    low = [p for p in range(15) if p % 2 == parity]
    return both([(device_index(z, p, c), device_index(z, p + 1, c)) for z in range(8) for p in low for c in range(2)])


def core_index():
    return lax.axis_index("c")


def row_block():
    x, y = lax.axis_index("xh") * 2 + lax.axis_index("xl"), lax.axis_index("y")
    return y * 4 + jnp.where(y % 2 == 1, 3 - x, x)


def rows():
    return lax.broadcasted_iota(jnp.int32, (8, 128), 0)


def lanes():
    return lax.broadcasted_iota(jnp.int32, (8, 128), 1)


def among(index, members):
    mask = index == members[0]
    for member in members[1:]:
        mask = mask | (index == member)
    return mask


def roll(tile, amount):
    amount %= 8
    return tile if amount == 0 else pltpu.roll(tile, amount, 0)


def mul_const(re, im, cr, ci):
    def axpy(a, x, b, y):
        terms = []
        for k, v in ((a, x), (b, y)):
            if abs(k) > 1e-12:
                terms.append((k, v))
        total = None
        for k, v in terms:
            if total is None:
                total = v if abs(k - 1) < 1e-12 else (-v if abs(k + 1) < 1e-12 else v * np.float32(k))
            elif abs(k - 1) < 1e-12:
                total = total + v
            elif abs(k + 1) < 1e-12:
                total = total - v
            else:
                total = total + v * np.float32(k)
        return total

    if abs(abs(cr) - abs(ci)) < 1e-12:
        root = np.float32(abs(cr))
        sr, si = math.copysign(1, cr), math.copysign(1, ci)
        return axpy(sr, re * root, -si, im * root), axpy(si, re * root, sr, im * root)
    return axpy(cr, re, -ci, im), axpy(ci, re, cr, im)


def rfft(x):
    n = len(x)
    if n == 2:
        return [(x[0] + x[1], None), (x[0] - x[1], None)]
    even, odd = rfft(x[0::2]), rfft(x[1::2])
    out = [None] * (n // 2 + 1)
    out[0] = (even[0][0] + odd[0][0], None)
    out[n // 2] = (even[0][0] - odd[0][0], None)
    out[n // 4] = (even[n // 4][0], -odd[n // 4][0])
    for k in range(1, n // 4):
        angle = -2 * math.pi * k / n
        tr, ti = mul_const(*odd[k], math.cos(angle), math.sin(angle))
        er, ei = even[k]
        out[k] = (er + tr, ei + ti)
        out[n // 2 - k] = (er - tr, ti - ei)
    return out


def irfft(spec):
    n = 2 * (len(spec) - 1)
    if n == 2:
        return [spec[0][0] + spec[1][0], spec[0][0] - spec[1][0]]
    q = n // 4
    even, odd = [None] * (q + 1), [None] * (q + 1)
    even[0] = (spec[0][0] + spec[2 * q][0], None)
    odd[0] = (spec[0][0] - spec[2 * q][0], None)
    even[q] = (2.0 * spec[q][0], None)
    odd[q] = (-2.0 * spec[q][1], None)
    for k in range(1, q):
        ar, ai = spec[k]
        br, bi = spec[2 * q - k]
        even[k] = (ar + br, ai - bi)
        angle = 2 * math.pi * k / n
        odd[k] = mul_const(ar - br, ai + bi, math.cos(angle), math.sin(angle))
    a, b = irfft(even), irfft(odd)
    return [v for two in zip(a, b) for v in two]


def split_kernel(src, out):
    for f in range(FIELDS):
        for t in range(2):
            for core in range(2):
                for pos in range(16):
                    out[level_index(pos, core), f, t] = src[f, t, core, pl.ds(8 * pos, 8), :]


def join_kernel(src, out, whole, sems):
    copies = []
    for f in range(FIELDS):
        for t in range(2):
            for core in range(2):
                for pos in range(16):
                    whole[f, t, core, pl.ds(8 * pos, 8), :] = src[level_index(pos, core), f, t]
        copies.append(pltpu.make_async_copy(whole.at[f], out.at[f], sems.at[f]))
        copies[-1].start()
    for copy in copies:
        copy.wait()


(A, AE, AW, AN, AS, AH, AC, GE, GW, GN, GS, GH, G, KE, KW, KN, KS, KH, KZ, DN, DS, DH) = range(22)


def coefficient_kernel(material, regions, coef, table, beside_table):
    pos = row_block()
    r, l = rows(), lanes()
    there = [l < 127, l > 0, (r < 7) | (pos < 15), (r > 0) | (pos > 0)]
    has_e, has_w = [jnp.where(t, 1.0, 0.0).astype(jnp.float32) for t in there[:2]]
    here = regions[pl.ds(8 * pos, 8), :]
    after = regions[pl.ds(8 * jnp.minimum(pos + 1, 15), 8), :]
    before = regions[pl.ds(8 * jnp.maximum(pos - 1, 0), 8), :]

    def value_of(row, classes):
        value = jnp.zeros((8, 128), jnp.float32)
        for m in range(4):
            value = jnp.where(classes == m, material[row, m], value)
        return value

    def faces(value, after, before, there):
        moved = [pltpu.roll(value, 127, 1), pltpu.roll(value, 1, 1), after, before]
        return [jnp.where(t, (value + v) * 0.5, value) for t, v in zip(there, moved)]

    def parts(row):
        v, va, vb = value_of(row, here), value_of(row, after), value_of(row, before)
        own = faces(v, roll(jnp.where(r == 0, va, v), 7), roll(jnp.where(r == 7, vb, v), 1), there)
        side = jnp.where(r == 0, roll(vb, 1), roll(va, 7))
        north = jnp.where(r == 0, v, roll(va, 6))
        south = jnp.where(r == 0, roll(vb, 2), v)
        always = l >= 0
        return v, own, side, faces(side, north, south, there[:2] + [always, always])

    shear, (se, sw, sn, ss), side_shear, side_shear_faces = parts(0)
    _, (ke, kw, kn, ks), _, side_kappa_faces = parts(1)
    axial, _, side_axial, _ = parts(2)
    a = 0.8 / (se + sw + sn + ss + 2.0 * shear)
    in_n, in_s = [jnp.where(t, 1.0, 0.0).astype(jnp.float32) for t in (r < 7, r > 0)]
    zero = jnp.zeros((8, 128), jnp.float32)

    def beside(south, north):
        return jnp.where(r == 0, south, jnp.where(r == 7, north, zero))

    g = 0.3 * a
    half_diag = 0.5 * (ke + kw + kn + ks + 2.0 * axial)
    total = side_shear_faces[0] + side_shear_faces[1] + side_shear_faces[2] + side_shear_faces[3]
    side_a = 0.8 / (total + 2.0 * side_shear)
    total = side_kappa_faces[0] + side_kappa_faces[1] + side_kappa_faces[2] + side_kappa_faces[3]
    side_half_diag = 0.5 * (total + 2.0 * side_axial)
    tiles = [
        a, a * se * has_e, a * sw * has_w, a * sn * in_n, a * ss * in_s, beside(a * ss, a * sn), a * shear,
        g * has_e, g * has_w, g * in_n, g * in_s, beside(-g, g), g,
        0.5 * ke * has_e, 0.5 * kw * has_w, 0.5 * kn * in_n, 0.5 * ks * in_s, beside(0.5 * ks, 0.5 * kn),
        0.5 * axial,
        0.3 * in_n, 0.3 * in_s, beside(zero - 0.3, zero + 0.3),
    ]
    for n, v in enumerate(tiles):
        coef[n] = v
    for q in range(PAIRS):
        m00, m11, m01 = 0.0, 2.0, 0.0
        if q:
            angle = 2 * math.pi * q / STEPS
            m00 = m11 = 1 - math.cos(angle)
            m01 = -math.sin(angle)
        d0, d1, di = half_diag + 0.5 * m00, half_diag + 0.5 * m11, -0.5 * m01
        inv = 0.8 / (d0 * d1 + di * di)
        for n, v in enumerate((zero + m00, zero + m11, zero + m01, inv * d1, inv * d0, inv * di)):
            table[q, n] = v
        d0, d1 = side_half_diag + 0.5 * m00, side_half_diag + 0.5 * m11
        inv = 0.8 / (d0 * d1 + di * di)
        for n, v in enumerate((side_a, inv * d1, inv * d0, inv * di)):
            beside_table[q, n] = v


def first_iterate(f, tiles, a, diagonal):
    re, im = tiles
    if f < 3:
        return a * re, a * im
    b00, b11, b01 = diagonal
    return b00 * re + b01 * im, b11 * im - b01 * re


TALL = 8 * 2 * FIELDS


def tile(j):
    return pl.ds(8 * j, 8)


def every(row):
    return pl.ds(row, 8, stride=8)


def send(q, block, row_a, row_b):
    even = (rows() * 0 + row_block() % 2) == 0
    for p in range(2):
        after, before = block[q, p, every(7), :], block[q, p, every(0), :]
        row_a[q, p] = jnp.where(even, after, before)
        row_b[q, p] = jnp.where(even, before, after)


def load(block, *place):
    return [[block[(*place, tile(2 * f + c), slice(None))] for c in range(2)] for f in range(FIELDS)]


def scaled(tiles, a, diagonal):
    return [first_iterate(f, tiles[f], a, diagonal) for f in range(FIELDS)]


def spectrum_kernel(src, x, outer, row_a, row_b):
    def body(f, _):
        for p in range(2):
            got = rfft([src[(t // 2) * 2 + p, f, t % 2] for t in range(STEPS)])
            pairs = [(got[0][0], got[16][0])] + got[1:16]
            for q in range(PAIRS):
                for c in range(2):
                    x[q, p, pl.ds(pl.multiple_of(16 * f, 16) + 8 * c, 8), :] = pairs[q][c]
        return 0

    lax.fori_loop(0, FIELDS, body, 0)

    def pair(q, _):
        outer[q] = x[q, core_index()]
        send(q, x, row_a, row_b)
        return 0

    lax.fori_loop(0, PAIRS, pair, 0, unroll=UNROLL)


def own_kernel(first, coef, table, x0, x, sib, part, start=None):
    l = lanes()
    east = jnp.where(l == 127, 0.0, 0.3).astype(jnp.float32)
    west = jnp.where(l == 0, 0.0, 0.3).astype(jnp.float32)
    core = core_index()
    first_core = (rows() * 0 + core) == 0
    sign = 1.0 - 2.0 * core.astype(jnp.float32)

    def pair(q, _):
        m00, m11, m01 = table[q, 0], table[q, 1], table[q, 2]
        pa, pb, pc = table[q, 3], table[q, 4], table[q, 5]
        beside = [load(sib, q, 0), load(sib, q, 1)]
        if first:
            beside = [scaled(tiles, coef[A], (pa, pb, pc)) for tiles in beside]
        for p, edge in ((core, True), (1 - core, False)):
            new = [[None, None] for _ in range(FIELDS)]
            div, flow = [None, None], [None, None]
            here = load(x, q, p)
            if first:
                here = scaled(here, coef[A], (pa, pb, pc))
                base = [[1.2 * here[f][c] for c in range(2)] for f in range(FIELDS)]
                for f in range(FIELDS):
                    for c in range(2):
                        start[q, p, tile(2 * f + c), :] = here[f][c]
            else:
                base = load(x0, q, p)
                base = [[base[f][c] + 0.2 * here[f][c] for c in range(2)] for f in range(FIELDS)]
            for c in range(2):
                cur = [here[f][c] for f in range(FIELDS)]
                es = [pltpu.roll(v, 127, 1) for v in cur]
                ws = [pltpu.roll(v, 1, 1) for v in cur]
                ns = [roll(v, 7) for v in cur]
                ss = [roll(v, 1) for v in cur]
                if edge:
                    total = [jnp.where(first_core, beside[0][f][c], beside[1][f][c]) for f in range(FIELDS)]
                    drop_u, drop_p = sign * total[2], sign * total[3]
                else:
                    dn = [beside[0][f][c] for f in range(FIELDS)]
                    up = [beside[1][f][c] for f in range(FIELDS)]
                    total = [u + d for u, d in zip(up, dn)]
                    drop_u, drop_p = up[2] - dn[2], up[3] - dn[3]
                grad = [
                    coef[GE] * es[3] - coef[GW] * ws[3],
                    coef[GN] * ns[3] - coef[GS] * ss[3],
                    coef[G] * drop_p,
                ]
                for f in range(3):
                    v = base[f][c] + coef[AE] * es[f] + coef[AW] * ws[f]
                    v = v + coef[AN] * ns[f] + coef[AS] * ss[f]
                    part[q, p, tile(2 * f + c), :] = v + coef[AC] * total[f] - grad[f]
                new[3][c] = base[3][c]
                flow[c] = (
                    coef[KE] * es[3]
                    + coef[KW] * ws[3]
                    + coef[KN] * ns[3]
                    + coef[KS] * ss[3]
                    + coef[KZ] * total[3]
                )
                div[c] = east * es[0] - west * ws[0] + coef[DN] * ns[1] - coef[DS] * ss[1] + 0.3 * drop_u
            g0 = flow[0] - (m00 * div[0] + m01 * div[1])
            g1 = flow[1] - (m11 * div[1] - m01 * div[0])
            part[q, p, tile(6), :] = new[3][0] + pa * g0 + pc * g1
            part[q, p, tile(7), :] = new[3][1] + pb * g1 - pc * g0
        return 0

    lax.fori_loop(0, PAIRS, pair, 0, unroll=UNROLL)


def own_first_kernel(coef, table, x, sib, part, start):
    own_kernel(True, coef, table, None, x, sib, part, start)


def finish(first, q, coef, table, beside_table, part, outer, row_a, row_b, edges):
    r = rows()
    core = core_index()
    sign = 2.0 * core.astype(jnp.float32) - 1.0
    even = (r * 0 + row_block() % 2) == 0
    m00, m11, m01 = table[q, 0], table[q, 1], table[q, 2]
    pa, pb, pc = table[q, 3], table[q, 4], table[q, 5]
    result = []
    for n, p, edge in ((0, core, True), (1, 1 - core, False)):
        a, b = row_a[q, p], row_b[q, p]
        edges[q % UNROLL, n, every(0), :] = jnp.where(even, b, a)
        edges[q % UNROLL, n, every(7), :] = jnp.where(even, a, b)
        new = [[None, None] for _ in range(FIELDS)]
        div, flow = [None, None], [None, None]
        side = load(edges, q % UNROLL, n)
        if first:
            side = scaled(side, beside_table[q, 0], [beside_table[q, m] for m in (1, 2, 3)])
        if edge:
            away = load(outer, q)
            if first:
                away = scaled(away, coef[A], (pa, pb, pc))
        for c in range(2):
            beside = [side[f][c] for f in range(FIELDS)]
            for f in range(3):
                new[f][c] = part[q, p, tile(2 * f + c), :] + coef[AH] * beside[f]
            new[1][c] = new[1][c] - coef[GH] * beside[3]
            flow[c] = coef[KH] * beside[3]
            div[c] = coef[DH] * beside[1]
            if edge:
                out = [away[f][c] for f in range(FIELDS)]
                for f in range(3):
                    new[f][c] = new[f][c] + coef[AC] * out[f]
                new[2][c] = new[2][c] - (sign * coef[G]) * out[3]
                flow[c] = flow[c] + coef[KZ] * out[3]
                div[c] = div[c] + (0.3 * sign) * out[2]
        g0 = flow[0] - (m00 * div[0] + m01 * div[1])
        g1 = flow[1] - (m11 * div[1] - m01 * div[0])
        new[3][0] = part[q, p, tile(6), :] + pa * g0 + pc * g1
        new[3][1] = part[q, p, tile(7), :] + pb * g1 - pc * g0
        result.append((p, new))
    return result


def clear(edges):
    edges[...] = jnp.zeros(edges.shape, jnp.float32)


def round_kernel(first, coef, table, beside_table, part, outer, row_a, row_b, y, next_outer, next_a, next_b, edges):
    clear(edges)

    def pair(q, _):
        for p, tiles in finish(first, q, coef, table, beside_table, part, outer, row_a, row_b, edges):
            for j in range(2 * FIELDS):
                y[q, p, tile(j), :] = tiles[j // 2][j % 2]
        next_outer[q] = y[q, core_index()]
        send(q, y, next_a, next_b)
        return 0

    lax.fori_loop(0, PAIRS, pair, 0, unroll=UNROLL)


def last_kernel(coef, table, beside_table, part, outer, row_a, row_b, out, y, edges):
    clear(edges)
    scale32 = np.float32(1.0 / STEPS)

    def pair(q, _):
        for p, tiles in finish(False, q, coef, table, beside_table, part, outer, row_a, row_b, edges):
            for j in range(2 * FIELDS):
                y[q, p, j // 2, j % 2] = tiles[j // 2][j % 2] * scale32
        return 0

    lax.fori_loop(0, PAIRS, pair, 0, unroll=UNROLL)

    def back(f, _):
        for p in range(2):
            spec = [(y[0, p, f, 0], None)]
            spec += [(y[q, p, f, 0], y[q, p, f, 1]) for q in range(1, PAIRS)]
            spec += [(y[0, p, f, 1], None)]
            for t, v in enumerate(irfft(spec)):
                out[(t // 2) * 2 + p, f, t % 2] = v
        return 0

    lax.fori_loop(0, FIELDS, back, 0)


def call(kernel, outs, in_spaces, scratch=(), limit=4, micros=1):
    f32 = jnp.float32
    shapes = [jax.ShapeDtypeStruct(s, f32) for s in outs]
    specs = [pl.BlockSpec(memory_space=pltpu.VMEM) for _ in outs]
    single = len(outs) == 1
    return pl.pallas_call(
        kernel,
        out_shape=shapes[0] if single else shapes,
        in_specs=[pl.BlockSpec(memory_space=m) for m in in_spaces],
        out_specs=specs[0] if single else specs,
        scratch_shapes=[pltpu.VMEM(s, f32) for s in scratch],
        compiler_params=pltpu.CompilerParams(vmem_limit_bytes=limit * MIB),
        cost_estimate=pl.CostEstimate(flops=0, bytes_accessed=int(micros * 3.69e6), transcendentals=0),
    )


def on_device(sources, regions, material):
    vmem, smem = pltpu.VMEM, pltpu.SMEM
    piece = (32, FIELDS, 2, 8, 128)
    block = (PAIRS, 2, TALL, 128)
    apart = (PAIRS, 2, FIELDS, 2, 8, 128)
    messages = [(PAIRS, TALL, 128), (PAIRS, 2, 8, 128), (PAIRS, 2, 8, 128)]
    edges = (UNROLL, 2, TALL, 128)

    def level(v):
        return lax.all_to_all(v, LEVEL, 0, 0, tiled=True)

    def exchange(v, outer, row_a, row_b):
        outer = lax.ppermute(outer, AXES, level_swap())
        sib = lax.ppermute(v, AXES, sibling_swap())
        row_a = lax.ppermute(row_a, AXES, row_swap(0))
        row_b = lax.ppermute(row_b, AXES, row_swap(1))
        return sib, outer, row_a, row_b

    whole = (FIELDS, 2, 2, 128, 128)
    arrived = level(call(split_kernel, [piece], [vmem])(sources))
    x, *out = call(spectrum_kernel, [block] + messages, [vmem], limit=8)(arrived)
    sib, *out = exchange(x, *out)
    x, regions, material = lax.optimization_barrier((x, regions, material))
    factors = call(coefficient_kernel, [(22, 8, 128), (PAIRS, 6, 8, 128), (PAIRS, 4, 8, 128)], [smem, vmem])(
        material, regions
    )
    coef, table, _ = factors
    part, x0 = call(own_first_kernel, [block] * 2, [vmem] * 4, limit=8, micros=2)(
        coef, table, x, sib
    )
    for n in range(2):
        x, *out = call(functools.partial(round_kernel, n == 0), [block] + messages, [vmem] * 7, [edges], 8)(
            *factors, part, *out
        )
        sib, *out = exchange(x, *out)
        part = call(functools.partial(own_kernel, False), [block], [vmem] * 5, limit=8, micros=2)(
            coef, table, x0, x, sib
        )
    answer = call(last_kernel, [piece], [vmem] * 7, [apart, edges], 8)(*factors, part, *out)
    return pl.pallas_call(
        join_kernel,
        out_shape=jax.ShapeDtypeStruct(whole, jnp.float32),
        in_specs=[pl.BlockSpec(memory_space=vmem)],
        out_specs=pl.BlockSpec(memory_space=pltpu.HBM),
        scratch_shapes=[pltpu.VMEM(whole, jnp.float32), pltpu.SemaphoreType.DMA((FIELDS,))],
        compiler_params=pltpu.CompilerParams(vmem_limit_bytes=4 * MIB),
    )(level(answer))


def solution(mesh):
    fine = Mesh(mesh.devices.reshape([SIZES[a] for a in AXES]), AXES)
    spec = P(None, ("xl", "y", "c"), ("z", "xh"), None, None)
    return jax.shard_map(
        on_device, mesh=fine, in_specs=(spec, P(), P()), out_specs=spec, check_vma=False
    )
```

```python
import functools
import math

import jax
import jax.numpy as jnp
import numpy as np
from jax import lax
from jax.experimental import pallas as pl
from jax.experimental.pallas import tpu as pltpu
from jax.sharding import Mesh
from jax.sharding import PartitionSpec as P

AXES = ("xl", "y", "c", "z", "xh")
SIZES = dict(xl=2, y=4, c=2, z=8, xh=2)
LEVEL = ("xl", "y", "c", "xh")
STEPS = 32
PAIRS = 16
FIELDS = 4
MIB = 1 << 20
UNROLL = 4


def chip_at(pos):
    y, x = divmod(pos, 4)
    return (3 - x if y % 2 else x), y


def level_index(pos, core):
    x, y = chip_at(pos)
    return ((((x % 2) * 4 + y) * 2 + core) * 2) + x // 2


def device_index(z, pos, core):
    x, y = chip_at(pos)
    return ((((x % 2) * 4 + y) * 2 + core) * 8 + z) * 2 + x // 2


def both(pairs):
    return pairs + [(t, s) for s, t in pairs]


def sibling_swap():
    return both([(device_index(z, p, 0), device_index(z, p, 1)) for z in range(8) for p in range(16)])


def level_swap():
    return both([(device_index(z, p, 1), device_index((z + 1) % 8, p, 0)) for z in range(8) for p in range(16)])


def row_swap(parity):
    low = range(parity, 16, 2)
    return both(
        [(device_index(z, p, c), device_index(z, (p + 1) % 16, c)) for z in range(8) for p in low for c in range(2)]
    )


def core_index():
    return lax.axis_index("c")


def row_block():
    x, y = lax.axis_index("xh") * 2 + lax.axis_index("xl"), lax.axis_index("y")
    return y * 4 + jnp.where(y % 2 == 1, 3 - x, x)


def rows():
    return lax.broadcasted_iota(jnp.int32, (8, 128), 0)


def lanes():
    return lax.broadcasted_iota(jnp.int32, (8, 128), 1)


def among(index, members):
    mask = index == members[0]
    for member in members[1:]:
        mask = mask | (index == member)
    return mask


def roll(tile, amount):
    amount %= 8
    return tile if amount == 0 else pltpu.roll(tile, amount, 0)


def mul_const(re, im, cr, ci):
    def axpy(a, x, b, y):
        terms = []
        for k, v in ((a, x), (b, y)):
            if abs(k) > 1e-12:
                terms.append((k, v))
        total = None
        for k, v in terms:
            if total is None:
                total = v if abs(k - 1) < 1e-12 else (-v if abs(k + 1) < 1e-12 else v * np.float32(k))
            elif abs(k - 1) < 1e-12:
                total = total + v
            elif abs(k + 1) < 1e-12:
                total = total - v
            else:
                total = total + v * np.float32(k)
        return total

    if abs(abs(cr) - abs(ci)) < 1e-12:
        root = np.float32(abs(cr))
        sr, si = math.copysign(1, cr), math.copysign(1, ci)
        return axpy(sr, re * root, -si, im * root), axpy(si, re * root, sr, im * root)
    return axpy(cr, re, -ci, im), axpy(ci, re, cr, im)


def rfft(x):
    n = len(x)
    if n == 2:
        return [(x[0] + x[1], None), (x[0] - x[1], None)]
    even, odd = rfft(x[0::2]), rfft(x[1::2])
    out = [None] * (n // 2 + 1)
    out[0] = (even[0][0] + odd[0][0], None)
    out[n // 2] = (even[0][0] - odd[0][0], None)
    out[n // 4] = (even[n // 4][0], -odd[n // 4][0])
    for k in range(1, n // 4):
        angle = -2 * math.pi * k / n
        tr, ti = mul_const(*odd[k], math.cos(angle), math.sin(angle))
        er, ei = even[k]
        out[k] = (er + tr, ei + ti)
        out[n // 2 - k] = (er - tr, ti - ei)
    return out


def irfft(spec):
    n = 2 * (len(spec) - 1)
    if n == 2:
        return [spec[0][0] + spec[1][0], spec[0][0] - spec[1][0]]
    q = n // 4
    even, odd = [None] * (q + 1), [None] * (q + 1)
    even[0] = (spec[0][0] + spec[2 * q][0], None)
    odd[0] = (spec[0][0] - spec[2 * q][0], None)
    even[q] = (2.0 * spec[q][0], None)
    odd[q] = (-2.0 * spec[q][1], None)
    for k in range(1, q):
        ar, ai = spec[k]
        br, bi = spec[2 * q - k]
        even[k] = (ar + br, ai - bi)
        angle = 2 * math.pi * k / n
        odd[k] = mul_const(ar - br, ai + bi, math.cos(angle), math.sin(angle))
    a, b = irfft(even), irfft(odd)
    return [v for two in zip(a, b) for v in two]


def split_kernel(src, out):
    for f in range(FIELDS):
        for t in range(2):
            for core in range(2):
                for pos in range(16):
                    out[level_index(pos, core), f, t] = src[f, t, core, pl.ds(8 * pos, 8), :]


def join_kernel(src, out, whole, sems):
    copies = []
    for f in range(FIELDS):
        for t in range(2):
            for core in range(2):
                for pos in range(16):
                    whole[f, t, core, pl.ds(8 * pos, 8), :] = src[level_index(pos, core), f, t]
        copies.append(pltpu.make_async_copy(whole.at[f], out.at[f], sems.at[f]))
        copies[-1].start()
    for copy in copies:
        copy.wait()


(A, AE, AW, AN, AS, AH, AC, GE, GW, GN, GS, GH, G, KE, KW, KN, KS, KH, KZ, DN, DS, DH) = range(22)


def coefficient_kernel(material, regions, coef, table, beside_table):
    pos = row_block()
    r, l = rows(), lanes()
    there = [l < 127, l > 0, (r < 7) | (pos < 15), (r > 0) | (pos > 0)]
    has_e, has_w = [jnp.where(t, 1.0, 0.0).astype(jnp.float32) for t in there[:2]]
    here = regions[pl.ds(8 * pos, 8), :]
    after = regions[pl.ds(8 * jnp.minimum(pos + 1, 15), 8), :]
    before = regions[pl.ds(8 * jnp.maximum(pos - 1, 0), 8), :]

    def value_of(row, classes):
        value = jnp.zeros((8, 128), jnp.float32)
        for m in range(4):
            value = jnp.where(classes == m, material[row, m], value)
        return value

    def faces(value, after, before, there):
        moved = [pltpu.roll(value, 127, 1), pltpu.roll(value, 1, 1), after, before]
        return [jnp.where(t, (value + v) * 0.5, value) for t, v in zip(there, moved)]

    def parts(row):
        v, va, vb = value_of(row, here), value_of(row, after), value_of(row, before)
        own = faces(v, roll(jnp.where(r == 0, va, v), 7), roll(jnp.where(r == 7, vb, v), 1), there)
        side = jnp.where(r == 0, roll(vb, 1), roll(va, 7))
        north = jnp.where(r == 0, v, roll(va, 6))
        south = jnp.where(r == 0, roll(vb, 2), v)
        always = l >= 0
        return v, own, side, faces(side, north, south, there[:2] + [always, always])

    shear, (se, sw, sn, ss), side_shear, side_shear_faces = parts(0)
    _, (ke, kw, kn, ks), _, side_kappa_faces = parts(1)
    axial, _, side_axial, _ = parts(2)
    a = 0.8 / (se + sw + sn + ss + 2.0 * shear)
    in_n, in_s = [jnp.where(t, 1.0, 0.0).astype(jnp.float32) for t in (r < 7, r > 0)]
    zero = jnp.zeros((8, 128), jnp.float32)

    def beside(south, north):
        return jnp.where((r == 0) & (pos > 0), south, jnp.where((r == 7) & (pos < 15), north, zero))

    g = 0.3 * a
    half_diag = 0.5 * (ke + kw + kn + ks + 2.0 * axial)
    total = side_shear_faces[0] + side_shear_faces[1] + side_shear_faces[2] + side_shear_faces[3]
    side_a = 0.8 / (total + 2.0 * side_shear)
    total = side_kappa_faces[0] + side_kappa_faces[1] + side_kappa_faces[2] + side_kappa_faces[3]
    side_half_diag = 0.5 * (total + 2.0 * side_axial)
    tiles = [
        a, a * se * has_e, a * sw * has_w, a * sn * in_n, a * ss * in_s, beside(a * ss, a * sn), a * shear,
        g * has_e, g * has_w, g * in_n, g * in_s, beside(-g, g), g,
        0.5 * ke * has_e, 0.5 * kw * has_w, 0.5 * kn * in_n, 0.5 * ks * in_s, beside(0.5 * ks, 0.5 * kn),
        0.5 * axial,
        0.3 * in_n, 0.3 * in_s, beside(zero - 0.3, zero + 0.3),
    ]
    for n, v in enumerate(tiles):
        coef[n] = v
    for q in range(PAIRS):
        m00, m11, m01 = 0.0, 2.0, 0.0
        if q:
            angle = 2 * math.pi * q / STEPS
            m00 = m11 = 1 - math.cos(angle)
            m01 = -math.sin(angle)
        d0, d1, di = half_diag + 0.5 * m00, half_diag + 0.5 * m11, -0.5 * m01
        inv = 0.8 / (d0 * d1 + di * di)
        for n, v in enumerate((zero + m00, zero + m11, zero + m01, inv * d1, inv * d0, inv * di)):
            table[q, n] = v
        d0, d1 = side_half_diag + 0.5 * m00, side_half_diag + 0.5 * m11
        inv = 0.8 / (d0 * d1 + di * di)
        for n, v in enumerate((side_a, inv * d1, inv * d0, inv * di)):
            beside_table[q, n] = v


def first_iterate(f, tiles, a, diagonal):
    re, im = tiles
    if f < 3:
        return a * re, a * im
    b00, b11, b01 = diagonal
    return b00 * re + b01 * im, b11 * im - b01 * re


TALL = 8 * 2 * FIELDS


def tile(j):
    return pl.ds(8 * j, 8)


def every(row):
    return pl.ds(row, 8, stride=8)


def send(q, block, row_a, row_b):
    even = (rows() * 0 + row_block() % 2) == 0
    for p in range(2):
        after, before = block[q, p, every(7), :], block[q, p, every(0), :]
        row_a[q, p] = jnp.where(even, after, before)
        row_b[q, p] = jnp.where(even, before, after)


def load(block, *place):
    return [[block[(*place, tile(2 * f + c), slice(None))] for c in range(2)] for f in range(FIELDS)]


def scaled(tiles, a, diagonal):
    return [first_iterate(f, tiles[f], a, diagonal) for f in range(FIELDS)]


def spectrum_kernel(src, x, outer, row_a, row_b):
    def body(f, _):
        for p in range(2):
            got = rfft([src[(t // 2) * 2 + p, f, t % 2] for t in range(STEPS)])
            pairs = [(got[0][0], got[16][0])] + got[1:16]
            for q in range(PAIRS):
                for c in range(2):
                    x[q, p, pl.ds(pl.multiple_of(16 * f, 16) + 8 * c, 8), :] = pairs[q][c]
        return 0

    lax.fori_loop(0, FIELDS, body, 0)

    def pair(q, _):
        outer[q] = x[q, core_index()]
        send(q, x, row_a, row_b)
        return 0

    lax.fori_loop(0, PAIRS, pair, 0, unroll=UNROLL)


def own_kernel(first, coef, table, x0, x, sib, part, start=None):
    l = lanes()
    east = jnp.where(l == 127, 0.0, 0.3).astype(jnp.float32)
    west = jnp.where(l == 0, 0.0, 0.3).astype(jnp.float32)
    core = core_index()
    first_core = (rows() * 0 + core) == 0
    sign = 1.0 - 2.0 * core.astype(jnp.float32)

    def pair(q, _):
        m00, m11, m01 = table[q, 0], table[q, 1], table[q, 2]
        pa, pb, pc = table[q, 3], table[q, 4], table[q, 5]
        beside = [load(sib, q, 0), load(sib, q, 1)]
        if first:
            beside = [scaled(tiles, coef[A], (pa, pb, pc)) for tiles in beside]
        for p, edge in ((core, True), (1 - core, False)):
            new = [[None, None] for _ in range(FIELDS)]
            div, flow = [None, None], [None, None]
            here = load(x, q, p)
            if first:
                here = scaled(here, coef[A], (pa, pb, pc))
                base = [[1.2 * here[f][c] for c in range(2)] for f in range(FIELDS)]
                for f in range(FIELDS):
                    for c in range(2):
                        start[q, p, tile(2 * f + c), :] = here[f][c]
            else:
                base = load(x0, q, p)
                base = [[base[f][c] + 0.2 * here[f][c] for c in range(2)] for f in range(FIELDS)]
            for c in range(2):
                cur = [here[f][c] for f in range(FIELDS)]
                es = [pltpu.roll(v, 127, 1) for v in cur]
                ws = [pltpu.roll(v, 1, 1) for v in cur]
                ns = [roll(v, 7) for v in cur]
                ss = [roll(v, 1) for v in cur]
                if edge:
                    total = [jnp.where(first_core, beside[0][f][c], beside[1][f][c]) for f in range(FIELDS)]
                    drop_u, drop_p = sign * total[2], sign * total[3]
                else:
                    dn = [beside[0][f][c] for f in range(FIELDS)]
                    up = [beside[1][f][c] for f in range(FIELDS)]
                    total = [u + d for u, d in zip(up, dn)]
                    drop_u, drop_p = up[2] - dn[2], up[3] - dn[3]
                grad = [
                    coef[GE] * es[3] - coef[GW] * ws[3],
                    coef[GN] * ns[3] - coef[GS] * ss[3],
                    coef[G] * drop_p,
                ]
                for f in range(3):
                    v = base[f][c] + coef[AE] * es[f] + coef[AW] * ws[f]
                    v = v + coef[AN] * ns[f] + coef[AS] * ss[f]
                    part[q, p, tile(2 * f + c), :] = v + coef[AC] * total[f] - grad[f]
                new[3][c] = base[3][c]
                flow[c] = (
                    coef[KE] * es[3]
                    + coef[KW] * ws[3]
                    + coef[KN] * ns[3]
                    + coef[KS] * ss[3]
                    + coef[KZ] * total[3]
                )
                div[c] = east * es[0] - west * ws[0] + coef[DN] * ns[1] - coef[DS] * ss[1] + 0.3 * drop_u
            g0 = flow[0] - (m00 * div[0] + m01 * div[1])
            g1 = flow[1] - (m11 * div[1] - m01 * div[0])
            part[q, p, tile(6), :] = new[3][0] + pa * g0 + pc * g1
            part[q, p, tile(7), :] = new[3][1] + pb * g1 - pc * g0
        return 0

    lax.fori_loop(0, PAIRS, pair, 0, unroll=UNROLL)


def own_first_kernel(coef, table, x, sib, part, start):
    own_kernel(True, coef, table, None, x, sib, part, start)


def finish(first, q, coef, table, beside_table, part, outer, row_a, row_b, edges):
    r = rows()
    core = core_index()
    sign = 2.0 * core.astype(jnp.float32) - 1.0
    here = jnp.where(lax.axis_index("z") == 7 * core, 0.0, 1.0).astype(jnp.float32)
    axial_u, axial_p, axial_g = here * coef[AC], here * coef[KZ], (here * sign) * coef[G]
    even = (r * 0 + row_block() % 2) == 0
    m00, m11, m01 = table[q, 0], table[q, 1], table[q, 2]
    pa, pb, pc = table[q, 3], table[q, 4], table[q, 5]
    result = []
    for n, p, edge in ((0, core, True), (1, 1 - core, False)):
        a, b = row_a[q, p], row_b[q, p]
        edges[q % UNROLL, n, every(0), :] = jnp.where(even, b, a)
        edges[q % UNROLL, n, every(7), :] = jnp.where(even, a, b)
        new = [[None, None] for _ in range(FIELDS)]
        div, flow = [None, None], [None, None]
        side = load(edges, q % UNROLL, n)
        if first:
            side = scaled(side, beside_table[q, 0], [beside_table[q, m] for m in (1, 2, 3)])
        if edge:
            away = load(outer, q)
            if first:
                away = scaled(away, coef[A], (pa, pb, pc))
        for c in range(2):
            beside = [side[f][c] for f in range(FIELDS)]
            for f in range(3):
                new[f][c] = part[q, p, tile(2 * f + c), :] + coef[AH] * beside[f]
            new[1][c] = new[1][c] - coef[GH] * beside[3]
            flow[c] = coef[KH] * beside[3]
            div[c] = coef[DH] * beside[1]
            if edge:
                out = [away[f][c] for f in range(FIELDS)]
                for f in range(3):
                    new[f][c] = new[f][c] + axial_u * out[f]
                new[2][c] = new[2][c] - axial_g * out[3]
                flow[c] = flow[c] + axial_p * out[3]
                div[c] = div[c] + (0.3 * here * sign) * out[2]
        g0 = flow[0] - (m00 * div[0] + m01 * div[1])
        g1 = flow[1] - (m11 * div[1] - m01 * div[0])
        new[3][0] = part[q, p, tile(6), :] + pa * g0 + pc * g1
        new[3][1] = part[q, p, tile(7), :] + pb * g1 - pc * g0
        result.append((p, new))
    return result


def clear(edges):
    edges[...] = jnp.zeros(edges.shape, jnp.float32)


def round_kernel(first, coef, table, beside_table, part, outer, row_a, row_b, y, next_outer, next_a, next_b, edges):
    clear(edges)

    def pair(q, _):
        for p, tiles in finish(first, q, coef, table, beside_table, part, outer, row_a, row_b, edges):
            for j in range(2 * FIELDS):
                y[q, p, tile(j), :] = tiles[j // 2][j % 2]
        next_outer[q] = y[q, core_index()]
        send(q, y, next_a, next_b)
        return 0

    lax.fori_loop(0, PAIRS, pair, 0, unroll=UNROLL)


def last_kernel(coef, table, beside_table, part, outer, row_a, row_b, out, y, edges):
    clear(edges)
    scale32 = np.float32(1.0 / STEPS)

    def pair(q, _):
        for p, tiles in finish(False, q, coef, table, beside_table, part, outer, row_a, row_b, edges):
            for j in range(2 * FIELDS):
                y[q, p, j // 2, j % 2] = tiles[j // 2][j % 2] * scale32
        return 0

    lax.fori_loop(0, PAIRS, pair, 0, unroll=UNROLL)

    def back(f, _):
        for p in range(2):
            spec = [(y[0, p, f, 0], None)]
            spec += [(y[q, p, f, 0], y[q, p, f, 1]) for q in range(1, PAIRS)]
            spec += [(y[0, p, f, 1], None)]
            for t, v in enumerate(irfft(spec)):
                out[(t // 2) * 2 + p, f, t % 2] = v
        return 0

    lax.fori_loop(0, FIELDS, back, 0)


def call(kernel, outs, in_spaces, scratch=(), limit=4, micros=1):
    f32 = jnp.float32
    shapes = [jax.ShapeDtypeStruct(s, f32) for s in outs]
    specs = [pl.BlockSpec(memory_space=pltpu.VMEM) for _ in outs]
    single = len(outs) == 1
    return pl.pallas_call(
        kernel,
        out_shape=shapes[0] if single else shapes,
        in_specs=[pl.BlockSpec(memory_space=m) for m in in_spaces],
        out_specs=specs[0] if single else specs,
        scratch_shapes=[pltpu.VMEM(s, f32) for s in scratch],
        compiler_params=pltpu.CompilerParams(vmem_limit_bytes=limit * MIB),
        cost_estimate=pl.CostEstimate(flops=0, bytes_accessed=int(micros * 3.69e6), transcendentals=0),
    )


def on_device(sources, regions, material):
    vmem, smem = pltpu.VMEM, pltpu.SMEM
    piece = (32, FIELDS, 2, 8, 128)
    block = (PAIRS, 2, TALL, 128)
    apart = (PAIRS, 2, FIELDS, 2, 8, 128)
    messages = [(PAIRS, TALL, 128), (PAIRS, 2, 8, 128), (PAIRS, 2, 8, 128)]
    edges = (UNROLL, 2, TALL, 128)

    def level(v):
        return lax.all_to_all(v, LEVEL, 0, 0, tiled=True)

    def exchange(v, outer, row_a, row_b):
        outer = lax.ppermute(outer, AXES, level_swap())
        sib = lax.ppermute(v, AXES, sibling_swap())
        row_a = lax.ppermute(row_a, AXES, row_swap(0))
        row_b = lax.ppermute(row_b, AXES, row_swap(1))
        return sib, outer, row_a, row_b

    whole = (FIELDS, 2, 2, 128, 128)
    arrived = level(call(split_kernel, [piece], [vmem])(sources))
    x, *out = call(spectrum_kernel, [block] + messages, [vmem], limit=8)(arrived)
    sib, *out = exchange(x, *out)
    x, regions, material = lax.optimization_barrier((x, regions, material))
    factors = call(coefficient_kernel, [(22, 8, 128), (PAIRS, 6, 8, 128), (PAIRS, 4, 8, 128)], [smem, vmem])(
        material, regions
    )
    coef, table, _ = factors
    part, x0 = call(own_first_kernel, [block] * 2, [vmem] * 4, limit=8, micros=2)(
        coef, table, x, sib
    )
    for n in range(2):
        x, *out = call(functools.partial(round_kernel, n == 0), [block] + messages, [vmem] * 7, [edges], 8)(
            *factors, part, *out
        )
        sib, *out = exchange(x, *out)
        part = call(functools.partial(own_kernel, False), [block], [vmem] * 5, limit=8, micros=2)(
            coef, table, x0, x, sib
        )
    answer = call(last_kernel, [piece], [vmem] * 7, [apart, edges], 8)(*factors, part, *out)
    return pl.pallas_call(
        join_kernel,
        out_shape=jax.ShapeDtypeStruct(whole, jnp.float32),
        in_specs=[pl.BlockSpec(memory_space=vmem)],
        out_specs=pl.BlockSpec(memory_space=pltpu.HBM),
        scratch_shapes=[pltpu.VMEM(whole, jnp.float32), pltpu.SemaphoreType.DMA((FIELDS,))],
        compiler_params=pltpu.CompilerParams(vmem_limit_bytes=4 * MIB),
    )(level(answer))


def solution(mesh):
    fine = Mesh(mesh.devices.reshape([SIZES[a] for a in AXES]), AXES)
    spec = P(None, ("xl", "y", "c"), ("z", "xh"), None, None)
    return jax.shard_map(
        on_device, mesh=fine, in_specs=(spec, P(), P()), out_specs=spec, check_vma=False
    )
```

```python
import functools
import math

import jax
import jax.numpy as jnp
import numpy as np
from jax import lax
from jax.experimental import pallas as pl
from jax.experimental.pallas import tpu as pltpu
from jax.sharding import Mesh
from jax.sharding import PartitionSpec as P

AXES = ("xl", "y", "c", "z", "xh")
SIZES = dict(xl=2, y=4, c=2, z=8, xh=2)
LEVEL = ("xl", "y", "c", "xh")
STEPS = 32
PAIRS = 16
FIELDS = 4
MIB = 1 << 20
UNROLL = 4


def chip_at(pos):
    y, x = divmod(pos, 4)
    return (3 - x if y % 2 else x), y


def level_index(pos, core):
    x, y = chip_at(pos)
    return ((((x % 2) * 4 + y) * 2 + core) * 2) + x // 2


def device_index(z, pos, core):
    x, y = chip_at(pos)
    return ((((x % 2) * 4 + y) * 2 + core) * 8 + z) * 2 + x // 2


def both(pairs):
    return pairs + [(t, s) for s, t in pairs]


def sibling_swap():
    return both([(device_index(z, p, 0), device_index(z, p, 1)) for z in range(8) for p in range(16)])


def level_swap():
    return both([(device_index(z, p, 1), device_index((z + 1) % 8, p, 0)) for z in range(8) for p in range(16)])


def row_swap(parity):
    low = range(parity, 16, 2)
    return both(
        [(device_index(z, p, c), device_index(z, (p + 1) % 16, c)) for z in range(8) for p in low for c in range(2)]
    )


def core_index():
    return lax.axis_index("c")


def row_block():
    x, y = lax.axis_index("xh") * 2 + lax.axis_index("xl"), lax.axis_index("y")
    return y * 4 + jnp.where(y % 2 == 1, 3 - x, x)


def rows():
    return lax.broadcasted_iota(jnp.int32, (8, 128), 0)


def lanes():
    return lax.broadcasted_iota(jnp.int32, (8, 128), 1)


def among(index, members):
    mask = index == members[0]
    for member in members[1:]:
        mask = mask | (index == member)
    return mask


def roll(tile, amount):
    amount %= 8
    return tile if amount == 0 else pltpu.roll(tile, amount, 0)


def mul_const(re, im, cr, ci):
    def axpy(a, x, b, y):
        terms = []
        for k, v in ((a, x), (b, y)):
            if abs(k) > 1e-12:
                terms.append((k, v))
        total = None
        for k, v in terms:
            if total is None:
                total = v if abs(k - 1) < 1e-12 else (-v if abs(k + 1) < 1e-12 else v * np.float32(k))
            elif abs(k - 1) < 1e-12:
                total = total + v
            elif abs(k + 1) < 1e-12:
                total = total - v
            else:
                total = total + v * np.float32(k)
        return total

    if abs(abs(cr) - abs(ci)) < 1e-12:
        root = np.float32(abs(cr))
        sr, si = math.copysign(1, cr), math.copysign(1, ci)
        return axpy(sr, re * root, -si, im * root), axpy(si, re * root, sr, im * root)
    return axpy(cr, re, -ci, im), axpy(ci, re, cr, im)


def rfft(x):
    n = len(x)
    if n == 2:
        return [(x[0] + x[1], None), (x[0] - x[1], None)]
    even, odd = rfft(x[0::2]), rfft(x[1::2])
    out = [None] * (n // 2 + 1)
    out[0] = (even[0][0] + odd[0][0], None)
    out[n // 2] = (even[0][0] - odd[0][0], None)
    out[n // 4] = (even[n // 4][0], -odd[n // 4][0])
    for k in range(1, n // 4):
        angle = -2 * math.pi * k / n
        tr, ti = mul_const(*odd[k], math.cos(angle), math.sin(angle))
        er, ei = even[k]
        out[k] = (er + tr, ei + ti)
        out[n // 2 - k] = (er - tr, ti - ei)
    return out


def irfft(spec):
    n = 2 * (len(spec) - 1)
    if n == 2:
        return [spec[0][0] + spec[1][0], spec[0][0] - spec[1][0]]
    q = n // 4
    even, odd = [None] * (q + 1), [None] * (q + 1)
    even[0] = (spec[0][0] + spec[2 * q][0], None)
    odd[0] = (spec[0][0] - spec[2 * q][0], None)
    even[q] = (2.0 * spec[q][0], None)
    odd[q] = (-2.0 * spec[q][1], None)
    for k in range(1, q):
        ar, ai = spec[k]
        br, bi = spec[2 * q - k]
        even[k] = (ar + br, ai - bi)
        angle = 2 * math.pi * k / n
        odd[k] = mul_const(ar - br, ai + bi, math.cos(angle), math.sin(angle))
    a, b = irfft(even), irfft(odd)
    return [v for two in zip(a, b) for v in two]


def split_kernel(src, out):
    for f in range(FIELDS):
        for t in range(2):
            for core in range(2):
                for pos in range(16):
                    out[level_index(pos, core), f, t] = src[f, t, core, pl.ds(8 * pos, 8), :]


def join_kernel(src, out, whole, sems):
    copies = []
    for f in range(FIELDS):
        for t in range(2):
            for core in range(2):
                for pos in range(16):
                    whole[f, t, core, pl.ds(8 * pos, 8), :] = src[level_index(pos, core), f, t]
        copies.append(pltpu.make_async_copy(whole.at[f], out.at[f], sems.at[f]))
        copies[-1].start()
    for copy in copies:
        copy.wait()


(A, AE, AW, AN, AS, AH, AC, GE, GW, GN, GS, GH, G, KE, KW, KN, KS, KH, KZ, DN, DS, DH) = range(22)


def coefficient_kernel(material, regions, coef, table, beside_table):
    pos = row_block()
    r, l = rows(), lanes()
    there = [l < 127, l > 0, (r < 7) | (pos < 15), (r > 0) | (pos > 0)]
    has_e, has_w = [jnp.where(t, 1.0, 0.0).astype(jnp.float32) for t in there[:2]]
    here = regions[pl.ds(8 * pos, 8), :]
    after = regions[pl.ds(8 * jnp.minimum(pos + 1, 15), 8), :]
    before = regions[pl.ds(8 * jnp.maximum(pos - 1, 0), 8), :]

    def value_of(row, classes):
        value = jnp.zeros((8, 128), jnp.float32)
        for m in range(4):
            value = jnp.where(classes == m, material[row, m], value)
        return value

    def faces(value, after, before, there):
        moved = [pltpu.roll(value, 127, 1), pltpu.roll(value, 1, 1), after, before]
        return [jnp.where(t, (value + v) * 0.5, value) for t, v in zip(there, moved)]

    def parts(row):
        v, va, vb = value_of(row, here), value_of(row, after), value_of(row, before)
        own = faces(v, roll(jnp.where(r == 0, va, v), 7), roll(jnp.where(r == 7, vb, v), 1), there)
        side = jnp.where(r == 0, roll(vb, 1), roll(va, 7))
        north = jnp.where(r == 0, v, roll(va, 6))
        south = jnp.where(r == 0, roll(vb, 2), v)
        always = l >= 0
        return v, own, side, faces(side, north, south, there[:2] + [always, always])

    shear, (se, sw, sn, ss), side_shear, side_shear_faces = parts(0)
    _, (ke, kw, kn, ks), _, side_kappa_faces = parts(1)
    axial, _, side_axial, _ = parts(2)
    a = 0.8 / (se + sw + sn + ss + 2.0 * shear)
    in_n, in_s = [jnp.where(t, 1.0, 0.0).astype(jnp.float32) for t in (r < 7, r > 0)]
    zero = jnp.zeros((8, 128), jnp.float32)

    def beside(south, north):
        return jnp.where((r == 0) & (pos > 0), south, jnp.where((r == 7) & (pos < 15), north, zero))

    g = 0.3 * a
    half_diag = 0.5 * (ke + kw + kn + ks + 2.0 * axial)
    total = side_shear_faces[0] + side_shear_faces[1] + side_shear_faces[2] + side_shear_faces[3]
    side_a = 0.8 / (total + 2.0 * side_shear)
    total = side_kappa_faces[0] + side_kappa_faces[1] + side_kappa_faces[2] + side_kappa_faces[3]
    side_half_diag = 0.5 * (total + 2.0 * side_axial)
    tiles = [
        a, a * se * has_e, a * sw * has_w, a * sn * in_n, a * ss * in_s, beside(a * ss, a * sn), a * shear,
        g * has_e, g * has_w, g * in_n, g * in_s, beside(-g, g), g,
        0.5 * ke * has_e, 0.5 * kw * has_w, 0.5 * kn * in_n, 0.5 * ks * in_s, beside(0.5 * ks, 0.5 * kn),
        0.5 * axial,
        0.3 * in_n, 0.3 * in_s, beside(zero - 0.3, zero + 0.3),
    ]
    for n, v in enumerate(tiles):
        coef[n] = v
    for q in range(PAIRS):
        m00, m11, m01 = 0.0, 2.0, 0.0
        if q:
            angle = 2 * math.pi * q / STEPS
            m00 = m11 = 1 - math.cos(angle)
            m01 = -math.sin(angle)
        d0, d1, di = half_diag + 0.5 * m00, half_diag + 0.5 * m11, -0.5 * m01
        inv = 0.8 / (d0 * d1 + di * di)
        for n, v in enumerate((zero + m00, zero + m11, zero + m01, inv * d1, inv * d0, inv * di)):
            table[q, n] = v
        d0, d1 = side_half_diag + 0.5 * m00, side_half_diag + 0.5 * m11
        inv = 0.8 / (d0 * d1 + di * di)
        for n, v in enumerate((side_a, inv * d1, inv * d0, inv * di)):
            beside_table[q, n] = v


def first_iterate(f, tiles, a, diagonal):
    re, im = tiles
    if f < 3:
        return a * re, a * im
    b00, b11, b01 = diagonal
    return b00 * re + b01 * im, b11 * im - b01 * re


TALL = 8 * 2 * FIELDS


def tile(j):
    return pl.ds(8 * j, 8)


def every(row):
    return pl.ds(row, 8, stride=8)


def send(q, block, row_a, row_b):
    even = (rows() * 0 + row_block() % 2) == 0
    for p in range(2):
        after, before = block[q, p, every(7), :], block[q, p, every(0), :]
        row_a[q, p] = jnp.where(even, after, before)
        row_b[q, p] = jnp.where(even, before, after)


def load(block, *place):
    return [[block[(*place, tile(2 * f + c), slice(None))] for c in range(2)] for f in range(FIELDS)]


def scaled(tiles, a, diagonal):
    return [first_iterate(f, tiles[f], a, diagonal) for f in range(FIELDS)]


def spectrum_kernel(src, x, outer, row_a, row_b):
    def body(f, _):
        for p in range(2):
            got = rfft([src[(t // 2) * 2 + p, f, t % 2] for t in range(STEPS)])
            pairs = [(got[0][0], got[16][0])] + got[1:16]
            for q in range(PAIRS):
                for c in range(2):
                    x[q, p, pl.ds(pl.multiple_of(16 * f, 16) + 8 * c, 8), :] = pairs[q][c]
        return 0

    lax.fori_loop(0, FIELDS, body, 0)

    def pair(q, _):
        outer[q] = x[q, core_index()]
        send(q, x, row_a, row_b)
        return 0

    lax.fori_loop(0, PAIRS, pair, 0, unroll=UNROLL)


def own_kernel(first, coef, table, x0, x, sib, part, start=None):
    l = lanes()
    east = jnp.where(l == 127, 0.0, 0.3).astype(jnp.float32)
    west = jnp.where(l == 0, 0.0, 0.3).astype(jnp.float32)
    core = core_index()
    first_core = (rows() * 0 + core) == 0
    sign = 1.0 - 2.0 * core.astype(jnp.float32)

    def pair(q, _):
        m00, m11, m01 = table[q, 0], table[q, 1], table[q, 2]
        pa, pb, pc = table[q, 3], table[q, 4], table[q, 5]
        beside = [load(sib, q, 0), load(sib, q, 1)]
        if first:
            beside = [scaled(tiles, coef[A], (pa, pb, pc)) for tiles in beside]
        for p, edge in ((core, True), (1 - core, False)):
            new = [[None, None] for _ in range(FIELDS)]
            div, flow = [None, None], [None, None]
            here = load(x, q, p)
            if first:
                here = scaled(here, coef[A], (pa, pb, pc))
                base = [[1.2 * here[f][c] for c in range(2)] for f in range(FIELDS)]
                for f in range(FIELDS):
                    for c in range(2):
                        start[q, p, tile(2 * f + c), :] = here[f][c]
            else:
                base = load(x0, q, p)
                base = [[base[f][c] + 0.2 * here[f][c] for c in range(2)] for f in range(FIELDS)]
            for c in range(2):
                cur = [here[f][c] for f in range(FIELDS)]
                es = [pltpu.roll(v, 127, 1) for v in cur]
                ws = [pltpu.roll(v, 1, 1) for v in cur]
                ns = [roll(v, 7) for v in cur]
                ss = [roll(v, 1) for v in cur]
                if edge:
                    total = [jnp.where(first_core, beside[0][f][c], beside[1][f][c]) for f in range(FIELDS)]
                    drop_u, drop_p = sign * total[2], sign * total[3]
                else:
                    dn = [beside[0][f][c] for f in range(FIELDS)]
                    up = [beside[1][f][c] for f in range(FIELDS)]
                    total = [u + d for u, d in zip(up, dn)]
                    drop_u, drop_p = up[2] - dn[2], up[3] - dn[3]
                grad = [
                    coef[GE] * es[3] - coef[GW] * ws[3],
                    coef[GN] * ns[3] - coef[GS] * ss[3],
                    coef[G] * drop_p,
                ]
                for f in range(3):
                    v = base[f][c] + coef[AE] * es[f] + coef[AW] * ws[f]
                    v = v + coef[AN] * ns[f] + coef[AS] * ss[f]
                    part[q, p, tile(2 * f + c), :] = v + coef[AC] * total[f] - grad[f]
                new[3][c] = base[3][c]
                flow[c] = (
                    coef[KE] * es[3]
                    + coef[KW] * ws[3]
                    + coef[KN] * ns[3]
                    + coef[KS] * ss[3]
                    + coef[KZ] * total[3]
                )
                div[c] = east * es[0] - west * ws[0] + coef[DN] * ns[1] - coef[DS] * ss[1] + 0.3 * drop_u
            g0 = flow[0] - (m00 * div[0] + m01 * div[1])
            g1 = flow[1] - (m11 * div[1] - m01 * div[0])
            part[q, p, tile(6), :] = new[3][0] + pa * g0 + pc * g1
            part[q, p, tile(7), :] = new[3][1] + pb * g1 - pc * g0
        return 0

    lax.fori_loop(0, PAIRS, pair, 0, unroll=UNROLL)


def own_first_kernel(coef, table, x, sib, part, start):
    own_kernel(True, coef, table, None, x, sib, part, start)


def finish(first, edge, q, coef, table, beside_table, part, row_a, row_b, sides, outer=None):
    core = core_index()
    p = core if edge else 1 - core
    here = jnp.where(lax.axis_index("z") == 7 * core, 0.0, 1.0).astype(jnp.float32)
    sign = here * (2.0 * core.astype(jnp.float32) - 1.0)
    even = (rows() * 0 + row_block() % 2) == 0
    m00, m11, m01 = table[q, 0], table[q, 1], table[q, 2]
    pa, pb, pc = table[q, 3], table[q, 4], table[q, 5]
    a, b = row_a[q, p], row_b[q, p]
    sides[q % UNROLL, every(0), :] = jnp.where(even, b, a)
    sides[q % UNROLL, every(7), :] = jnp.where(even, a, b)
    side = load(sides, q % UNROLL)
    if first:
        side = scaled(side, beside_table[q, 0], [beside_table[q, m] for m in (1, 2, 3)])
    if edge:
        away = load(outer, q)
        if first:
            away = scaled(away, coef[A], (pa, pb, pc))
    old = load(part, q, p)
    new = [[None, None] for _ in range(FIELDS)]
    div, flow = [None, None], [None, None]
    for c in range(2):
        for f in range(3):
            new[f][c] = old[f][c] + coef[AH] * side[f][c]
        new[1][c] = new[1][c] - coef[GH] * side[3][c]
        flow[c] = coef[KH] * side[3][c]
        div[c] = coef[DH] * side[1][c]
        if edge:
            for f in range(3):
                new[f][c] = new[f][c] + (here * coef[AC]) * away[f][c]
            new[2][c] = new[2][c] - (sign * coef[G]) * away[3][c]
            flow[c] = flow[c] + (here * coef[KZ]) * away[3][c]
            div[c] = div[c] + (0.3 * sign) * away[2][c]
    g0 = flow[0] - (m00 * div[0] + m01 * div[1])
    g1 = flow[1] - (m11 * div[1] - m01 * div[0])
    new[3][0] = old[3][0] + pa * g0 + pc * g1
    new[3][1] = old[3][1] + pb * g1 - pc * g0
    return new


def clear(sides):
    sides[...] = jnp.zeros(sides.shape, jnp.float32)


def other_kernel(first, coef, table, beside_table, part, row_a, row_b, y, sides):
    clear(sides)

    def pair(q, _):
        new = finish(first, False, q, coef, table, beside_table, part, row_a, row_b, sides)
        for j in range(2 * FIELDS):
            y[q, tile(j), :] = new[j // 2][j % 2]
        return 0

    lax.fori_loop(0, PAIRS, pair, 0, unroll=UNROLL)


def edge_kernel(first, coef, table, beside_table, part, outer, row_a, row_b, other, y, next_outer, next_a, next_b, sides):
    clear(sides)
    core = core_index()

    def pair(q, _):
        new = finish(first, True, q, coef, table, beside_table, part, row_a, row_b, sides, outer)
        for j in range(2 * FIELDS):
            y[q, core, tile(j), :] = new[j // 2][j % 2]
            next_outer[q, tile(j), :] = new[j // 2][j % 2]
        y[q, 1 - core] = other[q]
        send(q, y, next_a, next_b)
        return 0

    lax.fori_loop(0, PAIRS, pair, 0, unroll=UNROLL)


def to_steps(y, f):
    scale32 = np.float32(1.0 / STEPS)

    def at(q, c):
        return y[q, pl.ds(pl.multiple_of(16 * f, 16) + 8 * c, 8), :] * scale32

    return irfft([(at(0, 0), None)] + [(at(q, 0), at(q, 1)) for q in range(1, PAIRS)] + [(at(0, 1), None)])


def last_other_kernel(coef, table, beside_table, part, row_a, row_b, steps, y, sides):
    other_kernel(False, coef, table, beside_table, part, row_a, row_b, y, sides)

    def back(f, _):
        for t, v in enumerate(to_steps(y, f)):
            steps[f, t] = v
        return 0

    lax.fori_loop(0, FIELDS, back, 0)


def last_edge_kernel(coef, table, beside_table, part, outer, row_a, row_b, other, out, y, sides):
    clear(sides)
    core = core_index()

    def pair(q, _):
        new = finish(False, True, q, coef, table, beside_table, part, row_a, row_b, sides, outer)
        for j in range(2 * FIELDS):
            y[q, tile(j), :] = new[j // 2][j % 2]
        return 0

    lax.fori_loop(0, PAIRS, pair, 0, unroll=UNROLL)

    def back(f, _):
        for t, v in enumerate(to_steps(y, f)):
            out[(t // 2) * 2 + core, f, t % 2] = v
            out[(t // 2) * 2 + 1 - core, f, t % 2] = other[f, t]
        return 0

    lax.fori_loop(0, FIELDS, back, 0)


def call(kernel, outs, in_spaces, scratch=(), limit=4, micros=1):
    f32 = jnp.float32
    shapes = [jax.ShapeDtypeStruct(s, f32) for s in outs]
    specs = [pl.BlockSpec(memory_space=pltpu.VMEM) for _ in outs]
    single = len(outs) == 1
    return pl.pallas_call(
        kernel,
        out_shape=shapes[0] if single else shapes,
        in_specs=[pl.BlockSpec(memory_space=m) for m in in_spaces],
        out_specs=specs[0] if single else specs,
        scratch_shapes=[pltpu.VMEM(s, f32) for s in scratch],
        compiler_params=pltpu.CompilerParams(vmem_limit_bytes=limit * MIB),
        cost_estimate=pl.CostEstimate(flops=0, bytes_accessed=int(micros * 3.69e6), transcendentals=0),
    )


def on_device(sources, regions, material):
    vmem, smem = pltpu.VMEM, pltpu.SMEM
    piece = (32, FIELDS, 2, 8, 128)
    block = (PAIRS, 2, TALL, 128)
    plane = (PAIRS, TALL, 128)
    messages = [(PAIRS, TALL, 128), (PAIRS, 2, 8, 128), (PAIRS, 2, 8, 128)]
    sides = (UNROLL, TALL, 128)

    def level(v):
        return lax.all_to_all(v, LEVEL, 0, 0, tiled=True)

    def exchange(v, outer, row_a, row_b):
        outer = lax.ppermute(outer, AXES, level_swap())
        sib = lax.ppermute(v, AXES, sibling_swap())
        row_a = lax.ppermute(row_a, AXES, row_swap(0))
        row_b = lax.ppermute(row_b, AXES, row_swap(1))
        return sib, outer, row_a, row_b

    whole = (FIELDS, 2, 2, 128, 128)
    arrived = level(call(split_kernel, [piece], [vmem])(sources))
    x, *out = call(spectrum_kernel, [block] + messages, [vmem], limit=8)(arrived)
    sib, *out = exchange(x, *out)
    x, regions, material = lax.optimization_barrier((x, regions, material))
    factors = call(coefficient_kernel, [(22, 8, 128), (PAIRS, 6, 8, 128), (PAIRS, 4, 8, 128)], [smem, vmem])(
        material, regions
    )
    coef, table, _ = factors
    part, x0 = call(own_first_kernel, [block] * 2, [vmem] * 4, limit=8, micros=2)(
        coef, table, x, sib
    )
    for n in range(2):
        outer, *beside = out
        other = call(functools.partial(other_kernel, n == 0), [plane], [vmem] * 6, [sides], 8)(*factors, part, *beside)
        x, *out = call(functools.partial(edge_kernel, n == 0), [block] + messages, [vmem] * 8, [sides], 8)(
            *factors, part, outer, *beside, other
        )
        sib, *out = exchange(x, *out)
        part = call(functools.partial(own_kernel, False), [block], [vmem] * 5, limit=8, micros=2)(
            coef, table, x0, x, sib
        )
    outer, *beside = out
    other = call(last_other_kernel, [(FIELDS, STEPS, 8, 128)], [vmem] * 6, [plane, sides], 8)(*factors, part, *beside)
    answer = call(last_edge_kernel, [piece], [vmem] * 8, [plane, sides], 8)(*factors, part, outer, *beside, other)
    return pl.pallas_call(
        join_kernel,
        out_shape=jax.ShapeDtypeStruct(whole, jnp.float32),
        in_specs=[pl.BlockSpec(memory_space=vmem)],
        out_specs=pl.BlockSpec(memory_space=pltpu.HBM),
        scratch_shapes=[pltpu.VMEM(whole, jnp.float32), pltpu.SemaphoreType.DMA((FIELDS,))],
        compiler_params=pltpu.CompilerParams(vmem_limit_bytes=4 * MIB),
    )(level(answer))


def solution(mesh):
    fine = Mesh(mesh.devices.reshape([SIZES[a] for a in AXES]), AXES)
    spec = P(None, ("xl", "y", "c"), ("z", "xh"), None, None)
    return jax.shard_map(
        on_device, mesh=fine, in_specs=(spec, P(), P()), out_specs=spec, check_vma=False
    )
```

```python
import functools
import math

import jax
import jax.numpy as jnp
import numpy as np
from jax import lax
from jax.experimental import pallas as pl
from jax.experimental.pallas import tpu as pltpu
from jax.sharding import Mesh
from jax.sharding import PartitionSpec as P

AXES = ("xl", "y", "c", "z", "xh")
SIZES = dict(xl=2, y=4, c=2, z=8, xh=2)
LEVEL = ("xl", "y", "c", "xh")
STEPS = 32
PAIRS = 16
FIELDS = 4
MIB = 1 << 20
UNROLL = 4


def chip_at(pos):
    y, x = divmod(pos, 4)
    return (3 - x if y % 2 else x), y


def pos_of(x, y):
    return y * 4 + (3 - x if y % 2 else x)


def level_index(pos, core):
    x, y = chip_at(pos)
    return ((((x % 2) * 4 + y) * 2 + core) * 2) + x // 2


def device_index(z, pos, core):
    x, y = chip_at(pos)
    return ((((x % 2) * 4 + y) * 2 + core) * 8 + z) * 2 + x // 2


def both(pairs):
    return pairs + [(t, s) for s, t in pairs]


def sibling_swap():
    return both([(device_index(z, p, 0), device_index(z, p, 1)) for z in range(8) for p in range(16)])


def level_swap():
    pairs = [(device_index(z, p, 1), device_index(z + 1, p, 0)) for z in range(7) for p in range(16)]
    columns = [((x, y), (x, y + 1)) for x in range(3) for y in (0, 2)] + [((3, 1), (3, 2)), ((3, 3), (3, 0))]
    for z, core in ((0, 0), (7, 1)):
        for one, two in columns:
            pairs.append((device_index(z, pos_of(*one), core), device_index(z, pos_of(*two), core)))
    return both(pairs)


def row_swap(parity):
    low = range(parity, 16, 2)
    return both(
        [(device_index(z, p, c), device_index(z, (p + 1) % 16, c)) for z in range(8) for p in low for c in range(2)]
    )


def core_index():
    return lax.axis_index("c")


def row_block():
    x, y = lax.axis_index("xh") * 2 + lax.axis_index("xl"), lax.axis_index("y")
    return y * 4 + jnp.where(y % 2 == 1, 3 - x, x)


def rows():
    return lax.broadcasted_iota(jnp.int32, (8, 128), 0)


def lanes():
    return lax.broadcasted_iota(jnp.int32, (8, 128), 1)


def among(index, members):
    mask = index == members[0]
    for member in members[1:]:
        mask = mask | (index == member)
    return mask


def roll(tile, amount):
    amount %= 8
    return tile if amount == 0 else pltpu.roll(tile, amount, 0)


def mul_const(re, im, cr, ci):
    def axpy(a, x, b, y):
        terms = []
        for k, v in ((a, x), (b, y)):
            if abs(k) > 1e-12:
                terms.append((k, v))
        total = None
        for k, v in terms:
            if total is None:
                total = v if abs(k - 1) < 1e-12 else (-v if abs(k + 1) < 1e-12 else v * np.float32(k))
            elif abs(k - 1) < 1e-12:
                total = total + v
            elif abs(k + 1) < 1e-12:
                total = total - v
            else:
                total = total + v * np.float32(k)
        return total

    if abs(abs(cr) - abs(ci)) < 1e-12:
        root = np.float32(abs(cr))
        sr, si = math.copysign(1, cr), math.copysign(1, ci)
        return axpy(sr, re * root, -si, im * root), axpy(si, re * root, sr, im * root)
    return axpy(cr, re, -ci, im), axpy(ci, re, cr, im)


def rfft(x):
    n = len(x)
    if n == 2:
        return [(x[0] + x[1], None), (x[0] - x[1], None)]
    even, odd = rfft(x[0::2]), rfft(x[1::2])
    out = [None] * (n // 2 + 1)
    out[0] = (even[0][0] + odd[0][0], None)
    out[n // 2] = (even[0][0] - odd[0][0], None)
    out[n // 4] = (even[n // 4][0], -odd[n // 4][0])
    for k in range(1, n // 4):
        angle = -2 * math.pi * k / n
        tr, ti = mul_const(*odd[k], math.cos(angle), math.sin(angle))
        er, ei = even[k]
        out[k] = (er + tr, ei + ti)
        out[n // 2 - k] = (er - tr, ti - ei)
    return out


def irfft(spec):
    n = 2 * (len(spec) - 1)
    if n == 2:
        return [spec[0][0] + spec[1][0], spec[0][0] - spec[1][0]]
    q = n // 4
    even, odd = [None] * (q + 1), [None] * (q + 1)
    even[0] = (spec[0][0] + spec[2 * q][0], None)
    odd[0] = (spec[0][0] - spec[2 * q][0], None)
    even[q] = (2.0 * spec[q][0], None)
    odd[q] = (-2.0 * spec[q][1], None)
    for k in range(1, q):
        ar, ai = spec[k]
        br, bi = spec[2 * q - k]
        even[k] = (ar + br, ai - bi)
        angle = 2 * math.pi * k / n
        odd[k] = mul_const(ar - br, ai + bi, math.cos(angle), math.sin(angle))
    a, b = irfft(even), irfft(odd)
    return [v for two in zip(a, b) for v in two]


def split_kernel(src, out):
    for f in range(FIELDS):
        for t in range(2):
            for core in range(2):
                for pos in range(16):
                    out[level_index(pos, core), f, t] = src[f, t, core, pl.ds(8 * pos, 8), :]


def join_kernel(src, out, whole, sems):
    copies = []
    for f in range(FIELDS):
        for t in range(2):
            for core in range(2):
                for pos in range(16):
                    whole[f, t, core, pl.ds(8 * pos, 8), :] = src[level_index(pos, core), f, t]
        copies.append(pltpu.make_async_copy(whole.at[f], out.at[f], sems.at[f]))
        copies[-1].start()
    for copy in copies:
        copy.wait()


(A, AE, AW, AN, AS, AH, AC, GE, GW, GN, GS, GH, G, KE, KW, KN, KS, KH, KZ, DN, DS, DH) = range(22)


def coefficient_kernel(material, regions, coef, table, beside_table):
    pos = row_block()
    r, l = rows(), lanes()
    there = [l < 127, l > 0, (r < 7) | (pos < 15), (r > 0) | (pos > 0)]
    has_e, has_w = [jnp.where(t, 1.0, 0.0).astype(jnp.float32) for t in there[:2]]
    here = regions[pl.ds(8 * pos, 8), :]
    after = regions[pl.ds(8 * jnp.minimum(pos + 1, 15), 8), :]
    before = regions[pl.ds(8 * jnp.maximum(pos - 1, 0), 8), :]

    def value_of(row, classes):
        value = jnp.zeros((8, 128), jnp.float32)
        for m in range(4):
            value = jnp.where(classes == m, material[row, m], value)
        return value

    def faces(value, after, before, there):
        moved = [pltpu.roll(value, 127, 1), pltpu.roll(value, 1, 1), after, before]
        return [jnp.where(t, (value + v) * 0.5, value) for t, v in zip(there, moved)]

    def parts(row):
        v, va, vb = value_of(row, here), value_of(row, after), value_of(row, before)
        own = faces(v, roll(jnp.where(r == 0, va, v), 7), roll(jnp.where(r == 7, vb, v), 1), there)
        side = jnp.where(r == 0, roll(vb, 1), roll(va, 7))
        north = jnp.where(r == 0, v, roll(va, 6))
        south = jnp.where(r == 0, roll(vb, 2), v)
        always = l >= 0
        return v, own, side, faces(side, north, south, there[:2] + [always, always])

    shear, (se, sw, sn, ss), side_shear, side_shear_faces = parts(0)
    _, (ke, kw, kn, ks), _, side_kappa_faces = parts(1)
    axial, _, side_axial, _ = parts(2)
    a = 0.8 / (se + sw + sn + ss + 2.0 * shear)
    in_n, in_s = [jnp.where(t, 1.0, 0.0).astype(jnp.float32) for t in (r < 7, r > 0)]
    zero = jnp.zeros((8, 128), jnp.float32)

    def beside(south, north):
        return jnp.where((r == 0) & (pos > 0), south, jnp.where((r == 7) & (pos < 15), north, zero))

    g = 0.3 * a
    half_diag = 0.5 * (ke + kw + kn + ks + 2.0 * axial)
    total = side_shear_faces[0] + side_shear_faces[1] + side_shear_faces[2] + side_shear_faces[3]
    side_a = 0.8 / (total + 2.0 * side_shear)
    total = side_kappa_faces[0] + side_kappa_faces[1] + side_kappa_faces[2] + side_kappa_faces[3]
    side_half_diag = 0.5 * (total + 2.0 * side_axial)
    tiles = [
        a, a * se * has_e, a * sw * has_w, a * sn * in_n, a * ss * in_s, beside(a * ss, a * sn), a * shear,
        g * has_e, g * has_w, g * in_n, g * in_s, beside(-g, g), g,
        0.5 * ke * has_e, 0.5 * kw * has_w, 0.5 * kn * in_n, 0.5 * ks * in_s, beside(0.5 * ks, 0.5 * kn),
        0.5 * axial,
        0.3 * in_n, 0.3 * in_s, beside(zero - 0.3, zero + 0.3),
    ]
    for n, v in enumerate(tiles):
        coef[n] = v
    for q in range(PAIRS):
        m00, m11, m01 = 0.0, 2.0, 0.0
        if q:
            angle = 2 * math.pi * q / STEPS
            m00 = m11 = 1 - math.cos(angle)
            m01 = -math.sin(angle)
        d0, d1, di = half_diag + 0.5 * m00, half_diag + 0.5 * m11, -0.5 * m01
        inv = 0.8 / (d0 * d1 + di * di)
        for n, v in enumerate((zero + m00, zero + m11, zero + m01, inv * d1, inv * d0, inv * di)):
            table[q, n] = v
        d0, d1 = side_half_diag + 0.5 * m00, side_half_diag + 0.5 * m11
        inv = 0.8 / (d0 * d1 + di * di)
        for n, v in enumerate((side_a, inv * d1, inv * d0, inv * di)):
            beside_table[q, n] = v


def first_iterate(f, tiles, a, diagonal):
    re, im = tiles
    if f < 3:
        return a * re, a * im
    b00, b11, b01 = diagonal
    return b00 * re + b01 * im, b11 * im - b01 * re


TALL = 8 * 2 * FIELDS


def tile(j):
    return pl.ds(8 * j, 8)


def every(row):
    return pl.ds(row, 8, stride=8)


def send(q, block, row_a, row_b):
    even = (rows() * 0 + row_block() % 2) == 0
    for p in range(2):
        after, before = block[q, p, every(7), :], block[q, p, every(0), :]
        row_a[q, p] = jnp.where(even, after, before)
        row_b[q, p] = jnp.where(even, before, after)


def load(block, *place):
    return [[block[(*place, tile(2 * f + c), slice(None))] for c in range(2)] for f in range(FIELDS)]


def scaled(tiles, a, diagonal):
    return [first_iterate(f, tiles[f], a, diagonal) for f in range(FIELDS)]


def spectrum_kernel(src, x, outer, row_a, row_b):
    def body(f, _):
        for p in range(2):
            got = rfft([src[(t // 2) * 2 + p, f, t % 2] for t in range(STEPS)])
            pairs = [(got[0][0], got[16][0])] + got[1:16]
            for q in range(PAIRS):
                for c in range(2):
                    x[q, p, pl.ds(pl.multiple_of(16 * f, 16) + 8 * c, 8), :] = pairs[q][c]
        return 0

    lax.fori_loop(0, FIELDS, body, 0)

    def pair(q, _):
        outer[q] = x[q, core_index()]
        send(q, x, row_a, row_b)
        return 0

    lax.fori_loop(0, PAIRS, pair, 0, unroll=UNROLL)


def own_kernel(first, coef, table, x0, x, sib, part, start=None):
    l = lanes()
    east = jnp.where(l == 127, 0.0, 0.3).astype(jnp.float32)
    west = jnp.where(l == 0, 0.0, 0.3).astype(jnp.float32)
    core = core_index()
    first_core = (rows() * 0 + core) == 0
    sign = 1.0 - 2.0 * core.astype(jnp.float32)

    def pair(q, _):
        m00, m11, m01 = table[q, 0], table[q, 1], table[q, 2]
        pa, pb, pc = table[q, 3], table[q, 4], table[q, 5]
        beside = [load(sib, q, 0), load(sib, q, 1)]
        if first:
            beside = [scaled(tiles, coef[A], (pa, pb, pc)) for tiles in beside]
        for p, edge in ((core, True), (1 - core, False)):
            new = [[None, None] for _ in range(FIELDS)]
            div, flow = [None, None], [None, None]
            here = load(x, q, p)
            if first:
                here = scaled(here, coef[A], (pa, pb, pc))
                base = [[1.2 * here[f][c] for c in range(2)] for f in range(FIELDS)]
                for f in range(FIELDS):
                    for c in range(2):
                        start[q, p, tile(2 * f + c), :] = here[f][c]
            else:
                base = load(x0, q, p)
                base = [[base[f][c] + 0.2 * here[f][c] for c in range(2)] for f in range(FIELDS)]
            for c in range(2):
                cur = [here[f][c] for f in range(FIELDS)]
                es = [pltpu.roll(v, 127, 1) for v in cur]
                ws = [pltpu.roll(v, 1, 1) for v in cur]
                ns = [roll(v, 7) for v in cur]
                ss = [roll(v, 1) for v in cur]
                if edge:
                    total = [jnp.where(first_core, beside[0][f][c], beside[1][f][c]) for f in range(FIELDS)]
                    drop_u, drop_p = sign * total[2], sign * total[3]
                else:
                    dn = [beside[0][f][c] for f in range(FIELDS)]
                    up = [beside[1][f][c] for f in range(FIELDS)]
                    total = [u + d for u, d in zip(up, dn)]
                    drop_u, drop_p = up[2] - dn[2], up[3] - dn[3]
                grad = [
                    coef[GE] * es[3] - coef[GW] * ws[3],
                    coef[GN] * ns[3] - coef[GS] * ss[3],
                    coef[G] * drop_p,
                ]
                for f in range(3):
                    v = base[f][c] + coef[AE] * es[f] + coef[AW] * ws[f]
                    v = v + coef[AN] * ns[f] + coef[AS] * ss[f]
                    part[q, p, tile(2 * f + c), :] = v + coef[AC] * total[f] - grad[f]
                new[3][c] = base[3][c]
                flow[c] = (
                    coef[KE] * es[3]
                    + coef[KW] * ws[3]
                    + coef[KN] * ns[3]
                    + coef[KS] * ss[3]
                    + coef[KZ] * total[3]
                )
                div[c] = east * es[0] - west * ws[0] + coef[DN] * ns[1] - coef[DS] * ss[1] + 0.3 * drop_u
            g0 = flow[0] - (m00 * div[0] + m01 * div[1])
            g1 = flow[1] - (m11 * div[1] - m01 * div[0])
            part[q, p, tile(6), :] = new[3][0] + pa * g0 + pc * g1
            part[q, p, tile(7), :] = new[3][1] + pb * g1 - pc * g0
        return 0

    lax.fori_loop(0, PAIRS, pair, 0, unroll=UNROLL)


def own_first_kernel(coef, table, x, sib, part, start):
    own_kernel(True, coef, table, None, x, sib, part, start)


def finish(first, edge, q, coef, table, beside_table, part, row_a, row_b, sides, outer=None):
    core = core_index()
    p = core if edge else 1 - core
    here = jnp.where(lax.axis_index("z") == 7 * core, 0.0, 1.0).astype(jnp.float32)
    sign = here * (2.0 * core.astype(jnp.float32) - 1.0)
    even = (rows() * 0 + row_block() % 2) == 0
    m00, m11, m01 = table[q, 0], table[q, 1], table[q, 2]
    pa, pb, pc = table[q, 3], table[q, 4], table[q, 5]
    a, b = row_a[q, p], row_b[q, p]
    sides[q % UNROLL, every(0), :] = jnp.where(even, b, a)
    sides[q % UNROLL, every(7), :] = jnp.where(even, a, b)
    side = load(sides, q % UNROLL)
    if first:
        side = scaled(side, beside_table[q, 0], [beside_table[q, m] for m in (1, 2, 3)])
    if edge:
        away = load(outer, q)
        if first:
            away = scaled(away, coef[A], (pa, pb, pc))
    old = load(part, q, p)
    new = [[None, None] for _ in range(FIELDS)]
    div, flow = [None, None], [None, None]
    for c in range(2):
        for f in range(3):
            new[f][c] = old[f][c] + coef[AH] * side[f][c]
        new[1][c] = new[1][c] - coef[GH] * side[3][c]
        flow[c] = coef[KH] * side[3][c]
        div[c] = coef[DH] * side[1][c]
        if edge:
            for f in range(3):
                new[f][c] = new[f][c] + (here * coef[AC]) * away[f][c]
            new[2][c] = new[2][c] - (sign * coef[G]) * away[3][c]
            flow[c] = flow[c] + (here * coef[KZ]) * away[3][c]
            div[c] = div[c] + (0.3 * sign) * away[2][c]
    g0 = flow[0] - (m00 * div[0] + m01 * div[1])
    g1 = flow[1] - (m11 * div[1] - m01 * div[0])
    new[3][0] = old[3][0] + pa * g0 + pc * g1
    new[3][1] = old[3][1] + pb * g1 - pc * g0
    return new


def clear(sides):
    sides[...] = jnp.zeros(sides.shape, jnp.float32)


def other_kernel(first, coef, table, beside_table, part, row_a, row_b, y, sides):
    clear(sides)

    def pair(q, _):
        new = finish(first, False, q, coef, table, beside_table, part, row_a, row_b, sides)
        for j in range(2 * FIELDS):
            y[q, tile(j), :] = new[j // 2][j % 2]
        return 0

    lax.fori_loop(0, PAIRS, pair, 0, unroll=UNROLL)


def edge_kernel(first, coef, table, beside_table, part, outer, row_a, row_b, other, y, next_outer, next_a, next_b, sides):
    clear(sides)
    core = core_index()

    def pair(q, _):
        new = finish(first, True, q, coef, table, beside_table, part, row_a, row_b, sides, outer)
        for j in range(2 * FIELDS):
            y[q, core, tile(j), :] = new[j // 2][j % 2]
            next_outer[q, tile(j), :] = new[j // 2][j % 2]
        y[q, 1 - core] = other[q]
        send(q, y, next_a, next_b)
        return 0

    lax.fori_loop(0, PAIRS, pair, 0, unroll=UNROLL)


def to_steps(y, f):
    scale32 = np.float32(1.0 / STEPS)

    def at(q, c):
        return y[q, pl.ds(pl.multiple_of(16 * f, 16) + 8 * c, 8), :] * scale32

    return irfft([(at(0, 0), None)] + [(at(q, 0), at(q, 1)) for q in range(1, PAIRS)] + [(at(0, 1), None)])


def last_other_kernel(coef, table, beside_table, part, row_a, row_b, steps, y, sides):
    other_kernel(False, coef, table, beside_table, part, row_a, row_b, y, sides)

    def back(f, _):
        for t, v in enumerate(to_steps(y, f)):
            steps[f, t] = v
        return 0

    lax.fori_loop(0, FIELDS, back, 0)


def last_edge_kernel(coef, table, beside_table, part, outer, row_a, row_b, other, out, y, sides):
    clear(sides)
    core = core_index()

    def pair(q, _):
        new = finish(False, True, q, coef, table, beside_table, part, row_a, row_b, sides, outer)
        for j in range(2 * FIELDS):
            y[q, tile(j), :] = new[j // 2][j % 2]
        return 0

    lax.fori_loop(0, PAIRS, pair, 0, unroll=UNROLL)

    def back(f, _):
        for t, v in enumerate(to_steps(y, f)):
            out[(t // 2) * 2 + core, f, t % 2] = v
            out[(t // 2) * 2 + 1 - core, f, t % 2] = other[f, t]
        return 0

    lax.fori_loop(0, FIELDS, back, 0)


def call(kernel, outs, in_spaces, scratch=(), limit=4, micros=1):
    f32 = jnp.float32
    shapes = [jax.ShapeDtypeStruct(s, f32) for s in outs]
    specs = [pl.BlockSpec(memory_space=pltpu.VMEM) for _ in outs]
    single = len(outs) == 1
    return pl.pallas_call(
        kernel,
        out_shape=shapes[0] if single else shapes,
        in_specs=[pl.BlockSpec(memory_space=m) for m in in_spaces],
        out_specs=specs[0] if single else specs,
        scratch_shapes=[pltpu.VMEM(s, f32) for s in scratch],
        compiler_params=pltpu.CompilerParams(vmem_limit_bytes=limit * MIB),
        cost_estimate=pl.CostEstimate(flops=0, bytes_accessed=int(micros * 3.69e6), transcendentals=0),
    )


def on_device(sources, regions, material):
    vmem, smem = pltpu.VMEM, pltpu.SMEM
    piece = (32, FIELDS, 2, 8, 128)
    block = (PAIRS, 2, TALL, 128)
    plane = (PAIRS, TALL, 128)
    messages = [(PAIRS, TALL, 128), (PAIRS, 2, 8, 128), (PAIRS, 2, 8, 128)]
    sides = (UNROLL, TALL, 128)

    def level(v):
        return lax.all_to_all(v, LEVEL, 0, 0, tiled=True)

    def exchange(v, outer, row_a, row_b):
        outer = lax.ppermute(outer, AXES, level_swap())
        sib = lax.ppermute(v, AXES, sibling_swap())
        row_a = lax.ppermute(row_a, AXES, row_swap(0))
        row_b = lax.ppermute(row_b, AXES, row_swap(1))
        return sib, outer, row_a, row_b

    whole = (FIELDS, 2, 2, 128, 128)
    arrived = level(call(split_kernel, [piece], [vmem])(sources))
    x, *out = call(spectrum_kernel, [block] + messages, [vmem], limit=8)(arrived)
    sib, *out = exchange(x, *out)
    x, regions, material = lax.optimization_barrier((x, regions, material))
    factors = call(coefficient_kernel, [(22, 8, 128), (PAIRS, 6, 8, 128), (PAIRS, 4, 8, 128)], [smem, vmem])(
        material, regions
    )
    coef, table, _ = factors
    part, x0 = call(own_first_kernel, [block] * 2, [vmem] * 4, limit=8, micros=2)(
        coef, table, x, sib
    )
    for n in range(2):
        outer, *beside = out
        other = call(functools.partial(other_kernel, n == 0), [plane], [vmem] * 6, [sides], 8)(*factors, part, *beside)
        x, *out = call(functools.partial(edge_kernel, n == 0), [block] + messages, [vmem] * 8, [sides], 8)(
            *factors, part, outer, *beside, other
        )
        sib, *out = exchange(x, *out)
        part = call(functools.partial(own_kernel, False), [block], [vmem] * 5, limit=8, micros=2)(
            coef, table, x0, x, sib
        )
    outer, *beside = out
    other = call(last_other_kernel, [(FIELDS, STEPS, 8, 128)], [vmem] * 6, [plane, sides], 8)(*factors, part, *beside)
    answer = call(last_edge_kernel, [piece], [vmem] * 8, [plane, sides], 8)(*factors, part, outer, *beside, other)
    return pl.pallas_call(
        join_kernel,
        out_shape=jax.ShapeDtypeStruct(whole, jnp.float32),
        in_specs=[pl.BlockSpec(memory_space=vmem)],
        out_specs=pl.BlockSpec(memory_space=pltpu.HBM),
        scratch_shapes=[pltpu.VMEM(whole, jnp.float32), pltpu.SemaphoreType.DMA((FIELDS,))],
        compiler_params=pltpu.CompilerParams(vmem_limit_bytes=4 * MIB),
    )(level(answer))


def solution(mesh):
    fine = Mesh(mesh.devices.reshape([SIZES[a] for a in AXES]), AXES)
    spec = P(None, ("xl", "y", "c"), ("z", "xh"), None, None)
    return jax.shard_map(
        on_device, mesh=fine, in_specs=(spec, P(), P()), out_specs=spec, check_vma=False
    )
```
